256 devices in a mesh: section: 8 (over z), expert: 32 (over x, y, core).
Axes of the slice: x: 4, y: 4, z: 8, core: 2. Of those that a mesh axis runs over, the one named last changes fastest.
Arguments:
- out_grad: bfloat16 [8, 4096, 2560], P('section', 'expert'), may hold values from -6 to 6
- expert_ids: int32 [8, 4096], P('section', 'expert'), may hold values from 0 to 3, as said below
- slot_ids: int32 [8, 4096], P('section', 'expert'), may hold values from 0 to 32, as said below
- router_logits: float32 [8, 4096, 4], P('section', 'expert'), may hold values from -8 to 8
- saved_routed: bfloat16 [8, 32, 1056, 1024], P('section', 'expert'), may hold values from -6 to 6
- w_gate_up: bfloat16 [8, 32, 2560, 1024], P('section', 'expert'), may hold values from -0.125 to 0.125
- w_down: bfloat16 [8, 32, 512, 2560], P('section', 'expert'), may hold values from -0.09375 to 0.09375
- w_router: bfloat16 [8, 2560, 4], P('section'), may hold values from -0.125 to 0.125
Outputs:
- prev_grad: bfloat16 [8, 4096, 2560], P('section', 'expert')
- routed_hgrad: bfloat16 [8, 32, 1056, 1024], P('section', 'expert')
The draws below stay inside these ranges and needn't reach their ends.
Inputs may be any that keep to these rules, and one draw needn't show every extreme that they name: `expert_ids`: in each aligned block of 128 tokens of a section (one device's), one expert is named by exactly 33 tokens and every other expert by 1 to 32 tokens. `slot_ids`: within a block of 128 tokens, the number of earlier tokens of the block with the same expert.
All inputs are finite; a program needn't handle non-finite values.
Results may differ from the reference program's by a relative error of at most 0.0062.
Values may be sent and summed in bfloat16 or wider, within the bound.
A program may use at most 128 MiB of HBM per device.

```python
import jax
import jax.numpy as jnp
from jax import lax

D = 2560
FF = 4096
EXPERTS = 4
TOK_DEV = 128
SECTIONS = 8
GROUP = 8
FF_DEV = 512
TOKENS = 4096
MOST = 33
SLOTS = 1056
N_EXPERT = 32


def routing_tables(key):
    blocks = SECTIONS * TOKENS // TOK_DEV

    def one_block(block_index):
        block_key = jax.random.fold_in(key, block_index)
        keys = jax.random.split(block_key, 5)
        order = jax.random.permutation(keys[0], EXPERTS)
        first = jax.random.randint(keys[1], (), 0, EXPERTS)
        second = jax.random.randint(keys[2], (), 0, EXPERTS)
        hottest = order[first * second // EXPERTS]
        shuffled = jax.random.permutation(keys[3], TOK_DEV)
        ranking = jnp.zeros((TOK_DEV,), jnp.int32).at[shuffled].set(jnp.arange(TOK_DEV, dtype=jnp.int32))
        offset = jax.random.randint(keys[4], (), 0, EXPERTS - 1)
        spread = (ranking - MOST + offset) % (EXPERTS - 1)
        others = spread + (spread >= hottest).astype(jnp.int32)
        routes = jnp.where(ranking < MOST, hottest, others).astype(jnp.int32)
        onehot = (routes[:, None] == jnp.arange(EXPERTS, dtype=jnp.int32)[None, :]).astype(jnp.int32)
        places = jnp.sum((jnp.cumsum(onehot, axis=0) - onehot) * onehot, axis=1)
        return (routes, places.astype(jnp.int32))
    routes, places = jax.vmap(one_block)(jnp.arange(blocks, dtype=jnp.int32))
    return (routes.reshape(SECTIONS, TOKENS), places.reshape(SECTIONS, TOKENS))


def draw_expert_ids(key, part):
    return routing_tables(key)[0]


def draw_slot_ids(key, part):
    return routing_tables(key)[1]


def block_scale(own_key, dims, cuts, low, largest):
    def one(position, parts):
        draws = jax.random.uniform(jax.random.fold_in(jax.random.fold_in(own_key, 6), position), (parts,), jnp.float32, low / len(cuts), largest / len(cuts))
        return jnp.repeat(jnp.exp(draws), dims[position] // parts).reshape((-1,) + (1,) * (len(dims) - position - 1))

    gain = one(*cuts[0])
    for cut in cuts[1:]:
        gain = gain * one(*cut)
    return gain


def bell_draw(stream_key, extent, width, limit, cuts=(), kind=jnp.bfloat16):
    drawn = width * jax.random.normal(stream_key, extent, jnp.float32)
    if cuts:
        drawn = drawn * block_scale(stream_key, extent, cuts, -0.22, 0.18)
    return jnp.clip(drawn, -limit, limit).astype(kind)


def setup_inputs(seed: int = 0) -> dict:
    splits = jax.random.split(jax.random.key(seed), 9)
    out_grad = bell_draw(splits[0], (SECTIONS, TOKENS, D), 1.0, 6.0, ((0, 8), (1, 32)))
    expert_ids = draw_expert_ids(jax.random.fold_in(splits[8], 71), 0)
    slot_ids = draw_slot_ids(jax.random.fold_in(splits[8], 71), 0)
    router_logits = bell_draw(splits[3], (SECTIONS, TOKENS, EXPERTS), 2.0, 8.0, ((0, 8), (1, 32)), jnp.float32)
    saved_routed = bell_draw(splits[4], (SECTIONS, EXPERTS * GROUP, SLOTS, 2 * FF_DEV), 1.0, 6.0, ((0, 8), (1, 32)))
    w_gate_up = bell_draw(splits[5], (SECTIONS, EXPERTS * GROUP, D, 2 * FF_DEV), D ** -0.5, 0.125, ((0, 8), (1, 32)))
    w_down = bell_draw(splits[6], (SECTIONS, EXPERTS * GROUP, FF_DEV, D), FF ** -0.5, 0.09375, ((0, 8), (1, 32)))
    w_router = bell_draw(splits[7], (SECTIONS, D, EXPERTS), D ** -0.5, 0.125, ((0, 8),))
    return dict(out_grad=out_grad, expert_ids=expert_ids, slot_ids=slot_ids, router_logits=router_logits, saved_routed=saved_routed, w_gate_up=w_gate_up, w_down=w_down, w_router=w_router)


def silu_parts(gate_value):
    sigm = jax.nn.sigmoid(gate_value)
    return gate_value * sigm, sigm * (1.0 + gate_value * (1.0 - sigm))


def routed_backward(slot_rows, slot_score, kept, gate_up, down):
    half = down.shape[0]
    gate_value = kept[:, :half].astype(jnp.float32)
    up_value = kept[:, half:].astype(jnp.float32)
    activated, slope = silu_parts(gate_value)
    hidden = (activated * up_value).astype(jnp.bfloat16)
    expert_out = jnp.dot(hidden, down, preferred_element_type=jnp.float32)
    inner_dot = jnp.sum(slot_rows.astype(jnp.float32) * expert_out, axis=1).astype(jnp.bfloat16)
    hidden_grad = slot_score.astype(jnp.float32)[:, None] * lax.dot_general(
        slot_rows, down, (((1,), (1,)), ((), ())), preferred_element_type=jnp.float32)
    hidden_grads = jnp.concatenate([(hidden_grad * up_value * slope).astype(jnp.bfloat16),
                                    (hidden_grad * activated).astype(jnp.bfloat16)], axis=1)
    slot_dx = lax.dot_general(hidden_grads, gate_up, (((1,), (1,)), ((), ())),
                              preferred_element_type=jnp.float32).astype(jnp.bfloat16)
    return slot_dx, inner_dot, hidden_grads


def one_section(upstream, routes, places, logits, kept_routed, gate_up, down, router_weight):
    group = N_EXPERT // EXPERTS
    source = jnp.arange(TOKENS, dtype=jnp.int32) // TOK_DEV
    target = (routes * SLOTS + source * MOST + places).astype(jnp.int32)
    onehot = routes[:, None] == jnp.arange(EXPERTS, dtype=jnp.int32)[None, :]
    chosen = jnp.sum(jnp.where(onehot, logits, jnp.float32(0.0)), axis=1)
    gate_prob = jax.nn.sigmoid(chosen)
    gating = gate_prob.astype(jnp.bfloat16)
    slot_rows = jnp.zeros((EXPERTS * SLOTS, D), jnp.bfloat16).at[target].set(upstream).reshape(EXPERTS, SLOTS, D)
    slot_score = jnp.zeros((EXPERTS * SLOTS,), jnp.bfloat16).at[target].set(gating).reshape(EXPERTS, SLOTS)

    def per_piece(pieces):
        index, kept_piece, gate_piece, down_piece = pieces
        owner = (index // group).astype(jnp.int32)
        rows = lax.dynamic_index_in_dim(slot_rows, owner, 0, keepdims=False)
        scores = lax.dynamic_index_in_dim(slot_score, owner, 0, keepdims=False)
        return routed_backward(rows, scores, kept_piece, gate_piece, down_piece)

    slot_dx, inner_dot, hidden_grads = lax.map(per_piece, (
        jnp.arange(N_EXPERT, dtype=jnp.int32), kept_routed, gate_up, down))
    summed_dx = jnp.sum(slot_dx.astype(jnp.float32).reshape(EXPERTS, group, SLOTS, D), axis=1)
    summed_inner = jnp.sum(inner_dot.astype(jnp.float32).reshape(EXPERTS, group, SLOTS), axis=1)
    returned = summed_dx.reshape(EXPERTS * SLOTS, D)[target]
    inner_tok = summed_inner.reshape(EXPERTS * SLOTS)[target]
    dlogit = gate_prob * (1.0 - gate_prob) * inner_tok
    coeffs = jnp.where(onehot, dlogit[:, None], jnp.float32(0.0))
    router_dx = jnp.dot(coeffs, router_weight.astype(jnp.float32).T, precision=lax.Precision.HIGHEST)
    summed = (returned + router_dx).astype(jnp.bfloat16)
    return summed, hidden_grads


def reference(out_grad, expert_ids, slot_ids, router_logits, saved_routed, w_gate_up, w_down, w_router):
    grads, routed_list = [], []
    for section_index in range(SECTIONS):
        summed, routed_part = one_section(
            out_grad[section_index], expert_ids[section_index], slot_ids[section_index], router_logits[section_index],
            saved_routed[section_index], w_gate_up[section_index], w_down[section_index], w_router[section_index])
        grads.append(summed)
        routed_list.append(routed_part)
    stacked = jnp.stack(grads)
    previous = jnp.concatenate([stacked[1:], jnp.zeros_like(stacked[:1])], axis=0)
    return previous, jnp.stack(routed_list)
```

```python
import jax
import jax.numpy as jnp
from jax import lax
from jax.experimental import pallas as pl
from jax.experimental.pallas import tpu as pltpu
from jax.sharding import PartitionSpec as P

F32, BF16, I32 = jnp.float32, jnp.bfloat16, jnp.int32
SIDE = 4
TOK = 128
MOST = 33
REG = 32
D = 2560
FF_DEV = 512
SLOTS = 1056
QUART = D // 4
TILE_W = QUART + 128
WIN = 48

ORDER = [(0, 0), (0, 1), (0, 3), (0, 2), (3, 0), (1, 0), (3, 1), (1, 3), (2, 0), (1, 2), (2, 1), (2, 3), (3, 3), (2, 2), (3, 2), (1, 1)]
SLOT = {chunk: i for i, chunk in enumerate(ORDER)}
STEPS = 8
PLUS = (0, 1)


def packed(values):
    return sum(v << (2 * i) for i, v in enumerate(values))


PACK = [[packed([ORDER[2 * i + j][axis] for i in range(STEPS)]) for j in range(2)] for axis in range(2)]


def dot(a, b):
    return lax.dot_general(a, b, (((1,), (0,)), ((), ())), preferred_element_type=F32)


def dot_t(a, b):
    return lax.dot_general(a, b, (((1,), (1,)), ((), ())), preferred_element_type=F32)


def iota(shape, axis):
    return lax.broadcasted_iota(I32, shape, axis)


def onehot(mask):
    return jnp.where(mask, F32(1.0), F32(0.0)).astype(BF16)


def to_column(row, rows):
    mask = iota((rows, 128), 0) == iota((rows, 128), 1)
    return jnp.sum(jnp.where(mask, row, jnp.zeros((), row.dtype)), axis=1, keepdims=True)


def to_row(column):
    shape = (column.shape[0], 128)
    mask = iota(shape, 0) == iota(shape, 1)
    return jnp.sum(jnp.where(mask, column, jnp.zeros((), column.dtype)), axis=0, keepdims=True)


def backward(g, score, kept):
    gate_value, up_value = kept[:, :FF_DEV], kept[:, FF_DEV:]
    sigm = jax.nn.sigmoid(gate_value)
    activated = gate_value * sigm
    slope = sigm * (1.0 + gate_value * (1.0 - sigm))
    hidden = (activated * up_value).astype(BF16).astype(F32)
    inner = jnp.sum(hidden * g, axis=1, keepdims=True)
    hidden_grad = score * g
    hg = jnp.concatenate([hidden_grad * up_value * slope, hidden_grad * activated], axis=1).astype(BF16)
    return hg, inner


def kernel(sections, up_ref, ids_ref, slots_ref, logits_ref, router_ref, kept_hbm, wgu_hbm, wd_hbm,
           prev_ref, hgrad_hbm,
           kept_v, wgu_v, wd_v, hgo_v, x_v, xs_v, es_v, ein_v, eall_v, own_v, sbo_v, sbi_v, out_v,
           rel_v, dir_v, rto_v, rti_v, inn_v, fin_v, fino_v, ft_v, fto_v, rt_v, rts_v, hg_v, wrow_v, kex_v,
           send_sem, recv_sem, sb_send, sb_recv, loc_sem):
    sec = lax.axis_index("section")
    me = lax.axis_index("expert")
    c = lax.rem(me, 2)
    y = lax.rem(me // 2, SIDE)
    x = me // (2 * SIDE)

    def dev(dx=0, dy=0, dc=0, dz=0):
        s = lax.rem(sec + dz + sections, sections)
        e = (lax.rem(x + dx + SIDE, SIDE) * SIDE + lax.rem(y + dy + SIDE, SIDE)) * 2 + lax.rem(c + dc, 2)
        return (s, e)

    table = {}
    for d in (1, 3, 2):
        table["x", d] = (xs_v.at[d - 1], x_v.at[SLOT[0, d], 0], dev(dx=-d))
        table["e", d] = (es_v.at[d], ein_v.at[d - 1], dev(dx=-d))
    for d in range(4):
        n0 = SLOT[0, d]
        table["y+", d] = (x_v.at[n0, 0], x_v.at[SLOT[3, d], 0], dev(dy=1))
        table["y-", d] = (x_v.at[n0, 0], x_v.at[SLOT[1, d], 0], dev(dy=-1))
        if d in PLUS:
            table["yr", d] = (x_v.at[SLOT[3, d], 0], x_v.at[SLOT[2, d], 0], dev(dy=1))
            table["rr", d] = (out_v.at[SLOT[2, d]], rel_v.at[d], dev(dy=1))
        else:
            table["yr", d] = (x_v.at[SLOT[1, d], 0], x_v.at[SLOT[2, d], 0], dev(dy=-1))
            table["rr", d] = (out_v.at[SLOT[2, d]], rel_v.at[d], dev(dy=-1))
        for k in range(4):
            n = SLOT[k, d]
            table["sib", k, d] = (x_v.at[n, 0], x_v.at[n, 1], dev(dc=1))
        table["d+", d] = (out_v.at[SLOT[1, d]], dir_v.at[0, d], dev(dy=1))
        table["d-", d] = (out_v.at[SLOT[3, d]], dir_v.at[1, d], dev(dy=-1))
        table["f", d] = (fino_v.at[d], fin_v.at[d], dev(dx=d, dz=-1))
        table["ft", d] = (fto_v, ft_v.at[d], dev(dx=d, dz=-1))
    for i in range(1, 8):
        k, s = i // 2, i % 2
        j = 2 * ((4 - k) % 4) + s
        table["ea", i] = (eall_v.at[0], eall_v.at[j], dev(dy=k, dc=s))
        table["rt", i] = (rto_v.at[i], rti_v.at[j], dev(dy=k, dc=s))
    table[("ids",)] = (rts_v, rt_v, dev(dz=-1))
    number = {name: i for i, name in enumerate(table)}

    def copy(*name):
        src, dst, device = table[name]
        i = number[name]
        return pltpu.make_async_remote_copy(
            src_ref=src, dst_ref=dst, send_sem=send_sem.at[i], recv_sem=recv_sem.at[i],
            device_id=device, device_id_type=pl.DeviceIdType.MESH)

    def start(*name):
        copy(*name).start()

    def recv(*name):
        copy(*name).wait_recv()

    kept_copy = pltpu.make_async_copy(kept_hbm, kept_v, loc_sem.at[0])
    wd_copy = pltpu.make_async_copy(wd_hbm, wd_v, loc_sem.at[1])
    wgu_copy = pltpu.make_async_copy(wgu_hbm, wgu_v, loc_sem.at[2])
    wd_copy.start()
    kept_copy.start()
    wgu_copy.start()

    barrier = pltpu.get_barrier_semaphore()
    partners = [dev(dx=d) for d in (1, 2, 3)]
    partners += [dev(dy=k, dc=s) for k in range(4) for s in range(2) if k or s]
    partners += [dev(dx=d, dz=dz) for d in range(4) for dz in (-1, 1)]
    for partner in partners:
        pl.semaphore_signal(barrier, inc=1, device_id=partner, device_id_type=pl.DeviceIdType.MESH)

    ids_row, slot_row = ids_ref[...], slots_ref[...]
    rel_row = jnp.bitwise_and(x + SIDE - ids_row, 3)
    key = jnp.where(slot_row < REG, rel_row * REG + slot_row, -1)
    perm = onehot(iota((TOK, TOK), 0) == key)
    up = up_ref[...]
    rows = dot(perm, up).astype(BF16)
    x_v[SLOT[0, 0], 0] = rows[:REG]
    for d in range(1, 4):
        xs_v[d - 1] = rows[d * REG:(d + 1) * REG]
    ids_col, slot_col = to_column(ids_row, TOK), to_column(slot_row, TOK)
    chosen = jnp.sum(jnp.where(iota((TOK, SIDE), 1) == ids_col, logits_ref[...], 0.0), axis=1, keepdims=True)
    part = jax.nn.sigmoid(chosen)
    fold = jnp.zeros((4 * 16, QUART), F32)
    gates = jnp.zeros((4 * 16, 128), F32)
    for q in range(4):
        place = iota((4 * 16, TOK), 0) == rel_row * 17 + 4 * q
        fold += dot(onehot(place & (slot_row == REG)), up[:, q * QUART:(q + 1) * QUART])
        if q < 3:
            rounded = part.astype(BF16).astype(F32)
            spread = jnp.where(iota((TOK, 128), 1) == slot_col, rounded, 0.0).astype(BF16)
            gates += dot(onehot(place), spread)
            part = part - rounded
    tiles = jnp.concatenate([fold, gates], axis=1).astype(BF16)
    for d in range(4):
        es_v[d] = tiles[16 * d:16 * (d + 1)]
    rts_v[...] = jnp.concatenate([ids_row, slot_row, jnp.zeros((6, TOK), I32)], axis=0)

    pl.semaphore_wait(barrier, len(partners))
    for d in (1, 3):
        start("x", d)
    for d in (1, 2, 3):
        start("e", d)
    start("x", 2)
    start("y+", 0)
    start("y-", 0)
    start("sib", 0, 0)
    start("ids")

    chosen_expert = onehot(iota((8, SIDE), 1) == x)
    wrow_v[...] = dot_t(chosen_expert, router_ref[...])
    inn_v[...] = jnp.zeros_like(inn_v)

    @pl.loop(0, SLOTS // WIN)
    def _(i):
        hgo_v[pl.ds(pl.multiple_of(i * WIN, 16), WIN), :] = jnp.zeros((WIN, 2 * FF_DEV), BF16)

    for d in (1, 2, 3):
        recv("e", d)
    tile = es_v[0].astype(F32)
    for d in (1, 2, 3):
        tile += ein_v[d - 1].astype(F32)
    eall_v[0] = tile.astype(BF16)
    for i in range(1, 8):
        start("ea", i)

    def extra_row(shape, axis):
        r = iota(shape, axis)
        idx, d = r // 4, jnp.bitwise_and(r, 3)
        b = jnp.bitwise_and(x + d, 3) * 8 + jnp.bitwise_and(y + idx // 2, 3) * 2 + jnp.bitwise_and(c + idx, 1)
        return b * MOST + REG

    kept_copy.wait()

    def gather_kept(i, total):
        window = kept_v[pl.ds(pl.multiple_of(i * WIN, 16), WIN), :]
        return total + dot(onehot(iota((32, WIN), 1) + i * WIN == extra_row((32, WIN), 0)), window)

    kex_v[...] = lax.fori_loop(0, SLOTS // WIN, gather_kept, jnp.zeros((32, 2 * FF_DEV), F32))
    wd_copy.wait()
    wgu_copy.wait()

    before = [
        [("recv", "x", 1), ("start", "y+", 1), ("start", "sib", 0, 1), ("recv", "x", 3), ("start", "y-", 3), ("start", "sib", 0, 3)]
        + [("recv", "ea", i) for i in range(1, 8)],
        [("recv", "x", 2), ("start", "y-", 2), ("start", "sib", 0, 2),
         ("recv", "y+", 0), ("start", "yr", 0), ("start", "sib", 3, 0), ("recv", "y-", 0), ("start", "sib", 1, 0)],
        [("recv", "y+", 1), ("start", "yr", 1), ("start", "sib", 3, 1), ("recv", "y-", 3), ("start", "yr", 3), ("start", "sib", 1, 3),
         ("start", "y+", 3), ("start", "y+", 2)],
        [],
        [("recv", "y-", 2), ("start", "yr", 2), ("start", "sib", 1, 2), ("start", "y-", 1), ("recv", "yr", 0), ("start", "sib", 2, 0)],
        [("recv", "yr", 1), ("start", "sib", 2, 1), ("recv", "yr", 3), ("start", "sib", 2, 3)],
        [("recv", "y+", 3), ("start", "sib", 3, 3), ("recv", "yr", 2), ("start", "sib", 2, 2)],
        [("recv", "y+", 2), ("start", "sib", 3, 2), ("recv", "y-", 1), ("start", "sib", 1, 1)],
    ]
    after = [[], [], [("d-", 0)], [("d-", 1), ("d+", 3)], [("rr", 0), ("d+", 2)], [("rr", 1), ("rr", 3)], [("rr", 2)], []]

    def half_copy(n):
        return pltpu.make_async_remote_copy(
            src_ref=sbo_v.at[n], dst_ref=sbi_v.at[n], send_sem=sb_send.at[n], recv_sem=sb_recv.at[n],
            device_id=dev(dc=1), device_id_type=pl.DeviceIdType.MESH)

    def finish(m):
        for j in range(2):
            n = 2 * m + j
            half_copy(n).wait_recv()
            both = own_v[n] + sbi_v[n].astype(F32)
            own_v[n] = both
            out_v[n] = both.astype(BF16)

    @pl.loop(0, STEPS)
    def _(it):
        for i in range(STEPS):
            @pl.when(it == i)
            def _():
                for act, *name in before[i]:
                    (recv if act == "recv" else start)(*name)
                for j in range(2):
                    recv("sib", *ORDER[2 * i + j])

        rows = x_v[pl.ds(2 * it, 2)].reshape(4 * REG, D)
        g = dot_t(rows, wd_v[...])
        for j in range(2):
            k, d = [jnp.bitwise_and(jnp.right_shift(jnp.int32(PACK[axis][j]), 2 * it), 3) for axis in range(2)]
            for s in range(2):
                at = (2 * j + s) * REG
                idx = 2 * k + s
                first = (jnp.bitwise_and(x + d, 3) * 8 + jnp.bitwise_and(y + k, 3) * 2 + jnp.bitwise_and(c + s, 1)) * MOST
                base = pl.multiple_of(first // 16 * 16, 16)
                off = first - base
                window = pl.ds(base, WIN)
                kept = dot(onehot(iota((REG, WIN), 1) == iota((REG, WIN), 0) + off), kept_v[window, :])
                line = iota((16, 128), 0) == d
                score_row = jnp.sum(jnp.where(line, eall_v[idx, :, QUART:].astype(F32), 0.0), axis=0, keepdims=True)
                hg, inner = backward(g[at:at + REG], to_column(score_row, REG), kept)
                hg_v[at:at + REG, :] = hg
                inn_v[idx] = jnp.where(line, to_row(inner), inn_v[idx])
                placed = dot(onehot(iota((WIN, REG), 0) == iota((WIN, REG), 1) + off), hg)
                hgo_v[window, :] = (hgo_v[window, :].astype(F32) + placed).astype(BF16)
        for t in range(5):
            cols = slice(512 * t, 512 * (t + 1))
            dx = dot_t(hg_v[...], wgu_v[cols, :])
            for j in range(2):
                own_v[2 * it + j, :, cols] = dx[2 * j * REG:(2 * j + 1) * REG]
                sbo_v[2 * it + j, :, cols] = dx[(2 * j + 1) * REG:(2 * j + 2) * REG].astype(BF16)
        for j in range(2):
            half_copy(2 * it + j).start()

        @pl.when(it > 0)
        def _():
            finish(it - 1)
            for i in range(STEPS):
                if after[i]:
                    @pl.when(it - 1 == i)
                    def _():
                        for name in after[i]:
                            start(*name)

    finish(STEPS - 1)

    spread_tiles = eall_v[...].reshape(8 * 16, TILE_W)

    def select(q, flip):
        shape = (128, 32) if flip else (32, 128)
        r, place = iota(shape, 1 if flip else 0), iota(shape, 0 if flip else 1)
        return onehot(place == r // 4 * 16 + 4 * q + jnp.bitwise_and(r, 3))

    extra = jnp.concatenate([dot(select(q, False), spread_tiles[:, :QUART]).astype(BF16) for q in range(4)], axis=1)
    gate_rows = dot(select(0, False), spread_tiles[:, QUART:])
    score = jnp.sum(jnp.where(iota((32, 128), 1) == REG, gate_rows, 0.0), axis=1, keepdims=True)
    hg, inner = backward(dot_t(extra, wd_v[...]), score, kex_v[...])
    folded = jnp.zeros((8 * 16, QUART), F32)
    for q in range(4):
        folded += dot(select(q, True), dot_t(hg, wgu_v[q * QUART:(q + 1) * QUART, :]).astype(BF16))
    inner_at = jnp.where(iota((32, 128), 1) == REG, inner, 0.0).astype(BF16)
    inners = inn_v[...].reshape(8 * 16, 128) + dot(select(0, True), inner_at)
    rto_v[...] = jnp.concatenate([folded, inners], axis=1).astype(BF16).reshape(8, 16, TILE_W)
    for i in range(1, 8):
        start("rt", i)

    for d in (0, 3, 1, 2):
        recv("rr", d)
        n = SLOT[1 if d in PLUS else 3, d]
        out_v[n] = (own_v[n] + rel_v[d].astype(F32)).astype(BF16)
        start("d+" if d in PLUS else "d-", d)

    @pl.loop(0, SLOTS // WIN)
    def _(i):
        window = pl.ds(pl.multiple_of(i * WIN, 16), WIN)
        placed = dot(onehot(iota((WIN, 32), 0) + i * WIN == extra_row((WIN, 32), 1)), hg)
        hgo_v[window, :] = (hgo_v[window, :].astype(F32) + placed).astype(BF16)

    hgrad_copy = pltpu.make_async_copy(hgo_v, hgrad_hbm, loc_sem.at[3])
    hgrad_copy.start()

    total = rto_v[0].astype(F32)
    for i in range(1, 8):
        recv("rt", i)
    for i in range(1, 8):
        total += rti_v[i].astype(F32)
    gate_tile = eall_v[0, :, QUART:].astype(F32)
    kind = jnp.bitwise_and(iota((16, 128), 0), 3)
    terms = []
    for d in range(4):
        gate = jnp.sum(jnp.where(kind == d, gate_tile, 0.0), axis=0, keepdims=True)
        inner_row = jnp.sum(jnp.where(iota((16, 128), 0) == d, total[:, QUART:], 0.0), axis=0, keepdims=True)
        terms.append(gate * (1.0 - gate) * inner_row)
    all_terms = jnp.zeros((16, 128), F32)
    for d in range(4):
        all_terms = jnp.where(kind == d, terms[d], all_terms)
    last_term = jnp.sum(jnp.where(iota((16, 128), 1) == REG, all_terms, 0.0), axis=1, keepdims=True)
    w_row = wrow_v[0:1, :]
    w_fold = jnp.zeros((16, QUART), F32)
    for q in range(4):
        w_fold = jnp.where(iota((16, QUART), 0) // 4 == q, w_row[:, q * QUART:(q + 1) * QUART], w_fold)
    fto_v[...] = (total[:, :QUART] + last_term * w_fold).astype(BF16)
    for d in range(4):
        start("ft", d)
    for d in (0, 3, 1, 2):
        recv("d+", d)
        recv("d-", d)
        n = SLOT[0, d]
        rows = own_v[n] + dir_v[0, d].astype(F32) + dir_v[1, d].astype(F32)
        fino_v[d] = (rows + to_column(terms[d], REG) * w_row).astype(BF16)
        start("f", d)

    recv("ids")
    ids_col, slot_col = to_column(rt_v[0:1, :], TOK), to_column(rt_v[1:2, :], TOK)
    live = sec < sections - 1
    rel_col = jnp.bitwise_and(x + SIDE - ids_col, 3)
    back = onehot((iota((TOK, TOK), 1) == jnp.where(slot_col < REG, rel_col * REG + slot_col, -1)) & live)
    for d in range(4):
        recv("ft", d)
    for d in (0, 3, 1, 2):
        recv("f", d)
    fins = fin_v[...].reshape(TOK, D)
    fts = ft_v[...].reshape(4 * 16, QUART)
    for q in range(4):
        cols = slice(q * QUART, (q + 1) * QUART)
        pick = onehot((iota((TOK, 4 * 16), 1) == jnp.where(slot_col == REG, rel_col * 17 + 4 * q, -1)) & live)
        prev_ref[:, cols] = (dot(back, fins[:, cols]) + dot(pick, fts)).astype(BF16)

    for name in table:
        copy(*name).wait_send()
    for n in range(2 * STEPS):
        half_copy(n).wait_send()
    hgrad_copy.wait()


def on_device(out_grad, expert_ids, slot_ids, router_logits, saved_routed, w_gate_up, w_down, w_router):
    sections = lax.axis_size("section")
    vmem = pl.BlockSpec(memory_space=pltpu.VMEM)
    hbm = pl.BlockSpec(memory_space=pl.ANY)

    def body(*refs):
        kernel(sections, *refs)

    count = 3 + 3 + 4 * 10 + 16 + 14 + 1
    prev, hgrad = pl.pallas_call(
        body,
        out_shape=(jax.ShapeDtypeStruct((TOK, D), BF16), jax.ShapeDtypeStruct((SLOTS, 2 * FF_DEV), BF16)),
        in_specs=[vmem] * 5 + [hbm] * 3,
        out_specs=(vmem, hbm),
        scratch_shapes=[
            pltpu.VMEM((SLOTS, 2 * FF_DEV), BF16),
            pltpu.VMEM((D, 2 * FF_DEV), BF16),
            pltpu.VMEM((FF_DEV, D), BF16),
            pltpu.VMEM((SLOTS, 2 * FF_DEV), BF16),
            pltpu.VMEM((16, 2, REG, D), BF16),
            pltpu.VMEM((3, REG, D), BF16),
            pltpu.VMEM((4, 16, TILE_W), BF16),
            pltpu.VMEM((3, 16, TILE_W), BF16),
            pltpu.VMEM((8, 16, TILE_W), BF16),
            pltpu.VMEM((16, REG, D), F32),
            pltpu.VMEM((16, REG, D), BF16),
            pltpu.VMEM((16, REG, D), BF16),
            pltpu.VMEM((16, REG, D), BF16),
            pltpu.VMEM((4, REG, D), BF16),
            pltpu.VMEM((2, 4, REG, D), BF16),
            pltpu.VMEM((8, 16, TILE_W), BF16),
            pltpu.VMEM((8, 16, TILE_W), BF16),
            pltpu.VMEM((8, 16, 128), F32),
            pltpu.VMEM((4, REG, D), BF16),
            pltpu.VMEM((4, REG, D), BF16),
            pltpu.VMEM((4, 16, QUART), BF16),
            pltpu.VMEM((16, QUART), BF16),
            pltpu.VMEM((8, TOK), I32),
            pltpu.VMEM((8, TOK), I32),
            pltpu.VMEM((4 * REG, 2 * FF_DEV), BF16),
            pltpu.VMEM((8, D), F32),
            pltpu.VMEM((32, 2 * FF_DEV), F32),
            pltpu.SemaphoreType.DMA((count,)),
            pltpu.SemaphoreType.DMA((count,)),
            pltpu.SemaphoreType.DMA((16,)),
            pltpu.SemaphoreType.DMA((16,)),
            pltpu.SemaphoreType.DMA((4,)),
        ],
        compiler_params=pltpu.CompilerParams(collective_id=0, has_side_effects=True, vmem_limit_bytes=60 * 2**20),
        cost_estimate=pl.CostEstimate(flops=9 * 10**9, bytes_accessed=14 * 10**6, transcendentals=600000),
    )(out_grad[0], expert_ids, slot_ids, router_logits[0], w_router[0], saved_routed[0, 0], w_gate_up[0, 0], w_down[0, 0])
    return prev[None], hgrad[None, None]


def solution(mesh):
    placed = (
        P("section", "expert", None),
        P("section", "expert"),
        P("section", "expert"),
        P("section", "expert", None),
        P("section", "expert", None, None),
        P("section", "expert", None, None),
        P("section", "expert", None, None),
        P("section", None, None),
    )
    return jax.shard_map(
        on_device,
        mesh=mesh,
        in_specs=placed,
        out_specs=(P("section", "expert", None), P("section", "expert", None, None)),
        check_vma=False,
    )
```

```python
import jax
import jax.numpy as jnp
from jax import lax
from jax.experimental import pallas as pl
from jax.experimental.pallas import tpu as pltpu
from jax.sharding import PartitionSpec as P

F32, BF16, I32 = jnp.float32, jnp.bfloat16, jnp.int32
SIDE = 4
TOK = 128
MOST = 33
REG = 32
D = 2560
FF_DEV = 512
SLOTS = 1056
QUART = D // 4
TILE_W = QUART + 128
HALF = D // 2
PART = 528

ORDER = [(0, 0), (0, 1), (0, 3), (0, 2), (3, 0), (1, 0), (3, 1), (1, 3), (2, 0), (1, 2), (2, 1), (2, 3), (3, 3), (2, 2), (3, 2), (1, 1)]
SLOT = {chunk: i for i, chunk in enumerate(ORDER)}
STEPS = 8
PLUS = (0, 1)


def packed(values):
    return sum(v << (2 * i) for i, v in enumerate(values))


PACK = [[packed([ORDER[2 * i + j][axis] for i in range(STEPS)]) for j in range(2)] for axis in range(2)]


def dot(a, b):
    return lax.dot_general(a, b, (((1,), (0,)), ((), ())), preferred_element_type=F32)


def iota(shape, axis):
    return lax.broadcasted_iota(I32, shape, axis)


def onehot(mask):
    return jnp.where(mask, F32(1.0), F32(0.0)).astype(BF16)


def to_column(row, rows):
    mask = iota((rows, 128), 0) == iota((rows, 128), 1)
    return jnp.sum(jnp.where(mask, row, jnp.zeros((), row.dtype)), axis=1, keepdims=True)


def to_row(column):
    shape = (column.shape[0], 128)
    mask = iota(shape, 0) == iota(shape, 1)
    return jnp.sum(jnp.where(mask, column, jnp.zeros((), column.dtype)), axis=0, keepdims=True)


def backward(g, score, kept):
    gate_value, up_value = kept[:, :FF_DEV], kept[:, FF_DEV:]
    sigm = jax.nn.sigmoid(gate_value)
    activated = gate_value * sigm
    slope = sigm * (1.0 + gate_value * (1.0 - sigm))
    hidden = (activated * up_value).astype(BF16).astype(F32)
    inner = jnp.sum(hidden * g, axis=1, keepdims=True)
    hidden_grad = score * g
    hg = jnp.concatenate([hidden_grad * up_value * slope, hidden_grad * activated], axis=1).astype(BF16)
    return hg, inner


def kernel(sections, up_ref, ids_ref, slots_ref, logits_ref, router_ref, kept_hbm, wgu_hbm, wd_hbm,
           prev_ref, hgrad_hbm,
           kept_v, wgu_v, wd_v, wgut_v, wdt_v, perm_v, kp_v, hgp_v, x_v, xs_v, es_v, ein_v, eall_v, own_v, sbo_v, sbi_v, out_v,
           rel_v, dir_v, rto_v, rti_v, inn_v, fin_v, fino_v, ft_v, fto_v, rt_v, rts_v, hg_v,
           send_sem, recv_sem, sb_send, sb_recv, loc_sem):
    sec = lax.axis_index("section")
    me = lax.axis_index("expert")
    c = lax.rem(me, 2)
    y = lax.rem(me // 2, SIDE)
    x = me // (2 * SIDE)

    def dev(dx=0, dy=0, dc=0, dz=0):
        s = lax.rem(sec + dz + sections, sections)
        e = (lax.rem(x + dx + SIDE, SIDE) * SIDE + lax.rem(y + dy + SIDE, SIDE)) * 2 + lax.rem(c + dc, 2)
        return (s, e)

    table = {}
    for d in (1, 3, 2):
        table["x", d] = (xs_v.at[d - 1], x_v.at[SLOT[0, d], 0], dev(dx=-d))
        table["e", d] = (es_v.at[d], ein_v.at[d - 1], dev(dx=-d))
    for d in range(4):
        n0 = SLOT[0, d]
        table["y+", d] = (x_v.at[n0, 0], x_v.at[SLOT[3, d], 0], dev(dy=1))
        table["y-", d] = (x_v.at[n0, 0], x_v.at[SLOT[1, d], 0], dev(dy=-1))
        if d in PLUS:
            table["yr", d] = (x_v.at[SLOT[3, d], 0], x_v.at[SLOT[2, d], 0], dev(dy=1))
            table["rr", d] = (out_v.at[SLOT[2, d]], rel_v.at[d], dev(dy=1))
        else:
            table["yr", d] = (x_v.at[SLOT[1, d], 0], x_v.at[SLOT[2, d], 0], dev(dy=-1))
            table["rr", d] = (out_v.at[SLOT[2, d]], rel_v.at[d], dev(dy=-1))
        for k in range(4):
            n = SLOT[k, d]
            table["sib", k, d] = (x_v.at[n, 0], x_v.at[n, 1], dev(dc=1))
        for h in range(2):
            table["d+", d, h] = (out_v.at[SLOT[1, d], h], dir_v.at[0, d, h], dev(dy=1))
            table["d-", d, h] = (out_v.at[SLOT[3, d], h], dir_v.at[1, d, h], dev(dy=-1))
            table["f", d, h] = (fino_v.at[d, h], fin_v.at[d, h], dev(dx=d, dz=-1))
        table["ft", d] = (fto_v, ft_v.at[d], dev(dx=d, dz=-1))
    for i in range(1, 8):
        k, s = i // 2, i % 2
        j = 2 * ((4 - k) % 4) + s
        table["ea", i] = (eall_v.at[0], eall_v.at[j], dev(dy=k, dc=s))
        table["rt", i] = (rto_v.at[i], rti_v.at[j], dev(dy=k, dc=s))
    table[("ids",)] = (rts_v, rt_v, dev(dz=-1))
    number = {name: i for i, name in enumerate(table)}

    def copy(*name):
        src, dst, device = table[name]
        i = number[name]
        return pltpu.make_async_remote_copy(
            src_ref=src, dst_ref=dst, send_sem=send_sem.at[i], recv_sem=recv_sem.at[i],
            device_id=device, device_id_type=pl.DeviceIdType.MESH)

    def start(*name):
        copy(*name).start()

    def recv(*name):
        copy(*name).wait_recv()

    kept_copy = pltpu.make_async_copy(kept_hbm, kept_v, loc_sem.at[0])
    wd_copy = pltpu.make_async_copy(wd_hbm, wd_v, loc_sem.at[1])
    wgu_copy = pltpu.make_async_copy(wgu_hbm, wgu_v, loc_sem.at[2])
    wd_copy.start()
    kept_copy.start()
    wgu_copy.start()

    barrier = pltpu.get_barrier_semaphore()
    partners = [dev(dx=d) for d in (1, 2, 3)]
    partners += [dev(dy=k, dc=s) for k in range(4) for s in range(2) if k or s]
    partners += [dev(dx=d, dz=dz) for d in range(4) for dz in (-1, 1)]
    for partner in partners:
        pl.semaphore_signal(barrier, inc=1, device_id=partner, device_id_type=pl.DeviceIdType.MESH)

    ids_row, slot_row = ids_ref[...], slots_ref[...]
    rel_row = jnp.bitwise_and(x + SIDE - ids_row, 3)
    key = jnp.where(slot_row < REG, rel_row * REG + slot_row, -1)
    perm = onehot(iota((TOK, TOK), 0) == key)
    up = up_ref[...]
    rows = dot(perm, up).astype(BF16)
    x_v[SLOT[0, 0], 0] = rows[:REG]
    for d in range(1, 4):
        xs_v[d - 1] = rows[d * REG:(d + 1) * REG]
    ids_col, slot_col = to_column(ids_row, TOK), to_column(slot_row, TOK)
    chosen = jnp.sum(jnp.where(iota((SIDE, TOK), 0) == ids_row, logits_ref[...], 0.0), axis=0, keepdims=True)
    part = to_column(jax.nn.sigmoid(chosen), TOK)
    fold = jnp.zeros((4 * 16, QUART), F32)
    gates = jnp.zeros((4 * 16, 128), F32)
    for q in range(4):
        place = iota((4 * 16, TOK), 0) == rel_row * 17 + 4 * q
        fold += dot(onehot(place & (slot_row == REG)), up[:, q * QUART:(q + 1) * QUART])
        if q < 3:
            rounded = part.astype(BF16).astype(F32)
            spread = jnp.where(iota((TOK, 128), 1) == slot_col, rounded, 0.0).astype(BF16)
            gates += dot(onehot(place), spread)
            part = part - rounded
    tiles = jnp.concatenate([fold, gates], axis=1).astype(BF16)
    for d in range(4):
        es_v[d] = tiles[16 * d:16 * (d + 1)]
    rts_v[...] = jnp.concatenate([ids_row, slot_row, jnp.zeros((6, TOK), I32)], axis=0)

    def capacity(p):
        return jnp.where(p < 16 * REG, p // REG * MOST + jnp.bitwise_and(p, REG - 1), (p - 16 * REG) * MOST + REG)

    perm_v[...] = onehot(capacity(iota((PART, PART), 0)) == iota((PART, PART), 1))
    inn_v[...] = jnp.zeros_like(inn_v)
    pl.semaphore_wait(barrier, len(partners))
    for d in (1, 3):
        start("x", d)
    for d in (1, 2, 3):
        start("e", d)
    start("x", 2)
    start("y+", 0)
    start("y-", 0)
    start("sib", 0, 0)
    start("ids")

    wd_copy.wait()
    for t in range(5):
        wdt_v[512 * t:512 * (t + 1), :] = wd_v[:, 512 * t:512 * (t + 1)].T
    for d in (1, 2, 3):
        recv("e", d)
    tile = es_v[0].astype(F32)
    for d in (1, 2, 3):
        tile += ein_v[d - 1].astype(F32)
    eall_v[0] = tile.astype(BF16)
    for i in range(1, 8):
        start("ea", i)

    kept_copy.wait()
    for p in range(2):
        for t in range(2):
            cols = slice(512 * t, 512 * (t + 1))
            kp_v[p, :, cols] = dot(perm_v[...], kept_v[PART * p:PART * (p + 1), cols]).astype(BF16)
    perm_v[...] = onehot(capacity(iota((PART, PART), 1)) == iota((PART, PART), 0))
    for d, way in ((1, "y+"), (3, "y-")):
        recv("x", d)
        start(way, d)
        start("sib", 0, d)
    wgu_copy.wait()
    for t in range(5):
        wgut_v[:, 512 * t:512 * (t + 1)] = wgu_v[512 * t:512 * (t + 1), :].T

    before = [
        [("recv", "ea", 1)],
        [("recv", "y+", 0), ("start", "yr", 0), ("start", "sib", 3, 0), ("recv", "y-", 0), ("start", "sib", 1, 0),
         ("recv", "x", 2), ("start", "y-", 2), ("start", "sib", 0, 2)],
        [("recv", "y+", 1), ("start", "yr", 1), ("start", "sib", 3, 1), ("recv", "y-", 3), ("start", "yr", 3), ("start", "sib", 1, 3),
         ("start", "y+", 3), ("start", "y+", 2)]
        + [("recv", "ea", i) for i in range(2, 8)],
        [],
        [("recv", "y-", 2), ("start", "yr", 2), ("start", "sib", 1, 2), ("start", "y-", 1), ("recv", "yr", 0), ("start", "sib", 2, 0)],
        [("recv", "yr", 1), ("start", "sib", 2, 1), ("recv", "yr", 3), ("start", "sib", 2, 3)],
        [("recv", "y+", 3), ("start", "sib", 3, 3), ("recv", "yr", 2), ("start", "sib", 2, 2)],
        [("recv", "y+", 2), ("start", "sib", 3, 2), ("recv", "y-", 1), ("start", "sib", 1, 1)],
    ]
    after = [[], [], [], [], [("rr", 0)], [("rr", 1), ("rr", 3)], [("rr", 2)], []]

    def half_copy(n):
        return pltpu.make_async_remote_copy(
            src_ref=sbo_v.at[n], dst_ref=sbi_v.at[n], send_sem=sb_send.at[n], recv_sem=sb_recv.at[n],
            device_id=dev(dc=1), device_id_type=pl.DeviceIdType.MESH)

    def finish(m):
        for j in range(2):
            n = 2 * m + j
            half_copy(n).wait_recv()
            both = own_v[n] + sbi_v[n].astype(F32)
            own_v[n] = both
            out_v[n] = both.astype(BF16)

    @pl.loop(0, STEPS)
    def _(it):
        for i in range(STEPS):
            @pl.when(it == i)
            def _():
                for act, *name in before[i]:
                    (recv if act == "recv" else start)(*name)
                for j in range(2):
                    recv("sib", *ORDER[2 * i + j])

        rows = x_v[pl.ds(2 * it, 2)].reshape(4 * REG, D)
        g = dot(rows, wdt_v[...])
        for j in range(2):
            k, d = [jnp.bitwise_and(jnp.right_shift(jnp.int32(PACK[axis][j]), 2 * it), 3) for axis in range(2)]
            for s in range(2):
                at = (2 * j + s) * REG
                idx = 2 * k + s
                b = jnp.bitwise_and(x + d, 3) * 8 + jnp.bitwise_and(y + k, 3) * 2 + jnp.bitwise_and(c + s, 1)
                window = pl.ds(pl.multiple_of(jnp.bitwise_and(b, 15) * REG, REG), REG)
                kept = kp_v[b // 16, window, :].astype(F32)
                line = iota((16, 128), 0) == d
                score_row = jnp.sum(jnp.where(line, eall_v[idx, :, QUART:].astype(F32), 0.0), axis=0, keepdims=True)
                hg, inner = backward(g[at:at + REG], to_column(score_row, REG), kept)
                hg_v[at:at + REG, :] = hg
                inn_v[idx] = jnp.where(line, to_row(inner), inn_v[idx])
                hgp_v[b // 16, window, :] = hg
        for h in range(2):
            dx = dot(hg_v[...], wgut_v[:, HALF * h:HALF * (h + 1)])
            for j in range(2):
                own_v[2 * it + j, h] = dx[2 * j * REG:(2 * j + 1) * REG]
                sbo_v[2 * it + j, h] = dx[(2 * j + 1) * REG:(2 * j + 2) * REG].astype(BF16)
        for j in range(2):
            half_copy(2 * it + j).start()

        @pl.when(it > 0)
        def _():
            finish(it - 1)
            for i in range(STEPS):
                if after[i]:
                    @pl.when(it - 1 == i)
                    def _():
                        for name in after[i]:
                            start(*name)

    finish(STEPS - 1)

    def first_of(a, b, h):
        start("d+", b, h)
        start("d-", a, h)

    def second_of(a, b, h):
        for d, k, way in ((a, 1, "d+"), (b, 3, "d-")):
            n = SLOT[k, d]
            if h == 0:
                recv("rr", d)
            out_v[n, h] = (own_v[n, h] + rel_v[d, h].astype(F32)).astype(BF16)
            start(way, d, h)

    stages = [(0, 3, 0), (1, 2, 0), (0, 3, 1), (1, 2, 1)]
    first_of(*stages[0])

    spread_tiles = eall_v[...].reshape(8 * 16, TILE_W)

    def select(q, flip):
        shape = (128, 32) if flip else (32, 128)
        b, place = iota(shape, 1 if flip else 0), iota(shape, 0 if flip else 1)
        idx = 2 * jnp.bitwise_and(b // 2 - y + SIDE, 3) + jnp.bitwise_and(b + c, 1)
        return onehot(place == idx * 16 + 4 * q + jnp.bitwise_and(b // 8 - x + SIDE, 3))

    extra = jnp.concatenate([dot(select(q, False), spread_tiles[:, :QUART]).astype(BF16) for q in range(4)], axis=1)
    gate_rows = dot(select(0, False), spread_tiles[:, QUART:])
    score = jnp.sum(jnp.where(iota((32, 128), 1) == REG, gate_rows, 0.0), axis=1, keepdims=True)
    kept = kp_v[:, 16 * REG:, :].reshape(32, 2 * FF_DEV).astype(F32)
    hg, inner = backward(dot(extra, wdt_v[...]), score, kept)
    hgp_v[:, 16 * REG:, :] = hg.reshape(2, 16, 2 * FF_DEV)
    dx = dot(hg, wgut_v[...]).astype(BF16)
    folded = jnp.zeros((8 * 16, QUART), F32)
    for q in range(4):
        folded += dot(select(q, True), dx[:, q * QUART:(q + 1) * QUART])
    inner_at = jnp.where(iota((32, 128), 1) == REG, inner, 0.0).astype(BF16)
    inners = inn_v[...].reshape(8 * 16, 128) + dot(select(0, True), inner_at)
    rto_v[...] = jnp.concatenate([folded, inners], axis=1).astype(BF16).reshape(8, 16, TILE_W)
    for i in range(1, 8):
        start("rt", i)

    second_of(*stages[0])
    first_of(*stages[1])
    second_of(*stages[1])

    for p in range(2):
        for t in range(2):
            cols = slice(512 * t, 512 * (t + 1))
            kept_v[PART * p:PART * (p + 1), cols] = dot(perm_v[...], hgp_v[p, :, cols]).astype(BF16)
    hgrad_copy = pltpu.make_async_copy(kept_v, hgrad_hbm, loc_sem.at[3])
    hgrad_copy.start()

    total = rto_v[0].astype(F32)
    for i in range(1, 8):
        recv("rt", i)
    for i in range(1, 8):
        total += rti_v[i].astype(F32)
    gate_tile = eall_v[0, :, QUART:].astype(F32)
    kind = jnp.bitwise_and(iota((16, 128), 0), 3)
    terms = []
    for d in range(4):
        gate = jnp.sum(jnp.where(kind == d, gate_tile, 0.0), axis=0, keepdims=True)
        inner_row = jnp.sum(jnp.where(iota((16, 128), 0) == d, total[:, QUART:], 0.0), axis=0, keepdims=True)
        terms.append(gate * (1.0 - gate) * inner_row)
    all_terms = jnp.zeros((16, 128), F32)
    for d in range(4):
        all_terms = jnp.where(kind == d, terms[d], all_terms)
    last_term = jnp.sum(jnp.where(iota((16, 128), 1) == REG, all_terms, 0.0), axis=1, keepdims=True)
    w_row = jnp.sum(jnp.where(iota((SIDE, D), 0) == x, router_ref[...].astype(F32), 0.0), axis=0, keepdims=True)
    w_fold = jnp.zeros((16, QUART), F32)
    for q in range(4):
        w_fold = jnp.where(iota((16, QUART), 0) // 4 == q, w_row[:, q * QUART:(q + 1) * QUART], w_fold)
    fto_v[...] = (total[:, :QUART] + last_term * w_fold).astype(BF16)
    for d in range(4):
        start("ft", d)
    for i, (a, b, h) in enumerate(stages):
        for d in (b, a):
            recv("d+", d, h)
            recv("d-", d, h)
            n = SLOT[0, d]
            rows = own_v[n, h] + dir_v[0, d, h].astype(F32) + dir_v[1, d, h].astype(F32)
            fino_v[d, h] = (rows + to_column(terms[d], REG) * w_row[:, HALF * h:HALF * (h + 1)]).astype(BF16)
            start("f", d, h)
        if i + 2 < len(stages):
            first_of(*stages[i + 2])
            second_of(*stages[i + 2])

    recv("ids")
    ids_col, slot_col = to_column(rt_v[0:1, :], TOK), to_column(rt_v[1:2, :], TOK)
    live = sec < sections - 1
    rel_col = jnp.bitwise_and(x + SIDE - ids_col, 3)
    back = onehot((iota((TOK, TOK), 1) == jnp.where(slot_col < REG, rel_col * REG + slot_col, -1)) & live)
    for d in range(4):
        recv("ft", d)
    fts = ft_v[...].reshape(4 * 16, QUART)
    for h in range(2):
        for d in range(4):
            recv("f", d, h)
        whole = dot(back, fin_v[:, h].reshape(TOK, HALF))
        for q in (2 * h, 2 * h + 1):
            pick = onehot((iota((TOK, 4 * 16), 1) == jnp.where(slot_col == REG, rel_col * 17 + 4 * q, -1)) & live)
            at = (q - 2 * h) * QUART
            prev_ref[:, q * QUART:(q + 1) * QUART] = (whole[:, at:at + QUART] + dot(pick, fts)).astype(BF16)

    for name in table:
        copy(*name).wait_send()
    for n in range(2 * STEPS):
        half_copy(n).wait_send()
    hgrad_copy.wait()


def on_device(out_grad, expert_ids, slot_ids, router_logits, saved_routed, w_gate_up, w_down, w_router):
    sections = lax.axis_size("section")
    vmem = pl.BlockSpec(memory_space=pltpu.VMEM)
    hbm = pl.BlockSpec(memory_space=pl.ANY)

    def body(*refs):
        kernel(sections, *refs)

    count = 96
    prev, hgrad = pl.pallas_call(
        body,
        out_shape=(jax.ShapeDtypeStruct((TOK, D), BF16), jax.ShapeDtypeStruct((SLOTS, 2 * FF_DEV), BF16)),
        in_specs=[vmem] * 5 + [hbm] * 3,
        out_specs=(vmem, hbm),
        scratch_shapes=[
            pltpu.VMEM((SLOTS, 2 * FF_DEV), BF16),
            pltpu.VMEM((D, 2 * FF_DEV), BF16),
            pltpu.VMEM((FF_DEV, D), BF16),
            pltpu.VMEM((2 * FF_DEV, D), BF16),
            pltpu.VMEM((D, FF_DEV), BF16),
            pltpu.VMEM((PART, PART), BF16),
            pltpu.VMEM((2, PART, 2 * FF_DEV), BF16),
            pltpu.VMEM((2, PART, 2 * FF_DEV), BF16),
            pltpu.VMEM((16, 2, REG, D), BF16),
            pltpu.VMEM((3, REG, D), BF16),
            pltpu.VMEM((4, 16, TILE_W), BF16),
            pltpu.VMEM((3, 16, TILE_W), BF16),
            pltpu.VMEM((8, 16, TILE_W), BF16),
            pltpu.VMEM((16, 2, REG, HALF), F32),
            pltpu.VMEM((16, 2, REG, HALF), BF16),
            pltpu.VMEM((16, 2, REG, HALF), BF16),
            pltpu.VMEM((16, 2, REG, HALF), BF16),
            pltpu.VMEM((4, 2, REG, HALF), BF16),
            pltpu.VMEM((2, 4, 2, REG, HALF), BF16),
            pltpu.VMEM((8, 16, TILE_W), BF16),
            pltpu.VMEM((8, 16, TILE_W), BF16),
            pltpu.VMEM((8, 16, 128), F32),
            pltpu.VMEM((4, 2, REG, HALF), BF16),
            pltpu.VMEM((4, 2, REG, HALF), BF16),
            pltpu.VMEM((4, 16, QUART), BF16),
            pltpu.VMEM((16, QUART), BF16),
            pltpu.VMEM((8, TOK), I32),
            pltpu.VMEM((8, TOK), I32),
            pltpu.VMEM((4 * REG, 2 * FF_DEV), BF16),
            pltpu.SemaphoreType.DMA((count,)),
            pltpu.SemaphoreType.DMA((count,)),
            pltpu.SemaphoreType.DMA((16,)),
            pltpu.SemaphoreType.DMA((16,)),
            pltpu.SemaphoreType.DMA((4,)),
        ],
        compiler_params=pltpu.CompilerParams(collective_id=0, has_side_effects=True, vmem_limit_bytes=60 * 2**20),
        cost_estimate=pl.CostEstimate(flops=9 * 10**9, bytes_accessed=14 * 10**6, transcendentals=600000),
    )(out_grad[0], expert_ids, slot_ids, router_logits[0].T, w_router[0].T, saved_routed[0, 0], w_gate_up[0, 0], w_down[0, 0])
    return prev[None], hgrad[None, None]


def solution(mesh):
    placed = (
        P("section", "expert", None),
        P("section", "expert"),
        P("section", "expert"),
        P("section", "expert", None),
        P("section", "expert", None, None),
        P("section", "expert", None, None),
        P("section", "expert", None, None),
        P("section", None, None),
    )
    return jax.shard_map(
        on_device,
        mesh=mesh,
        in_specs=placed,
        out_specs=(P("section", "expert", None), P("section", "expert", None, None)),
        check_vma=False,
    )
```

```python
import jax
import jax.numpy as jnp
from jax import lax
from jax.experimental import pallas as pl
from jax.experimental.pallas import tpu as pltpu
from jax.sharding import PartitionSpec as P

F32, BF16, I32 = jnp.float32, jnp.bfloat16, jnp.int32
SIDE = 4
TOK = 128
MOST = 33
REG = 32
D = 2560
FF_DEV = 512
SLOTS = 1056
QUART = D // 4
TILE_W = QUART + 128
HALF = D // 2
PART = 528

ORDER = [
    (0, 0), (0, 1), (1, 3), (1, 0), (3, 0), (0, 2), (2, 0), (3, 1), (2, 1), (2, 3), (1, 2), (0, 3), (3, 3), (1, 1),
    (3, 2), (2, 2),
]
SLOT = {chunk: i for i, chunk in enumerate(ORDER)}
PLAN = [
    ("x", 1), ("x", 3), ("y+", 0), ("y-", 0), ("e", 1), ("sib", 0, 0), ("e", 3), ("e", 2), ("x", 2), ("prep",),
    ("sib", 0, 3), ("y+", 1), ("y-", 3), ("E0",), ("ea", 2), ("ea", 1), ("yr", 0), ("ea", 3), ("es", 0), ("y-", 2),
    ("sib", 0, 1), ("yr", 1), ("sib", 3, 1), ("y+", 3), ("sib", 1, 0), ("sib", 0, 2), ("yr", 3), ("es", 2), ("es", 3),
    ("y+", 2), ("es", 1), ("sib", 1, 3), ("sib", 3, 0), ("y-", 1), ("step", 0), ("step", 1), ("sib", 2, 0), ("yr", 2),
    ("sib", 1, 2), ("step", 2), ("ext",), ("sib", 2, 1), ("sib", 2, 3), ("step", 3), ("step", 4), ("sib", 1, 1),
    ("fin", 3), ("d-", 1, 0), ("rr", 0), ("sib", 3, 3), ("step", 5), ("fin", 2), ("d-", 1, 1), ("fin", 4), ("rr", 1),
    ("rr", 3), ("fin", 1), ("sib", 3, 2), ("sib", 2, 2), ("step", 6), ("step", 7), ("rs",), ("rt", 2), ("rt", 1),
    ("rt", 3), ("d-", 0, 1), ("fin", 6), ("fin", 0), ("d+", 0, 1), ("fin", 7), ("d+", 1, 0), ("rr", 2), ("d+", 1, 1),
    ("terms",), ("d-", 0, 0), ("ft",), ("d+", 0, 0), ("final", 0, 1), ("d+", 3, 1), ("d-", 3, 1), ("d-", 3, 0),
    ("d+", 3, 0), ("final", 1, 0), ("fin", 5), ("final", 1, 1), ("d-", 2, 1), ("final", 0, 0), ("d+", 2, 1),
    ("d-", 2, 0), ("d+", 2, 0), ("final", 3, 1), ("final", 3, 0), ("final", 2, 1), ("final", 2, 0), ("perm",),
    ("out", 1), ("out", 0),
]
STEPS = 8
PLUS = (0, 1)


def packed(values):
    return sum(v << (2 * i) for i, v in enumerate(values))


PACK = [[packed([ORDER[2 * i + j][axis] for i in range(STEPS)]) for j in range(2)] for axis in range(2)]


def dot(a, b):
    return lax.dot_general(a, b, (((1,), (0,)), ((), ())), preferred_element_type=F32)


def iota(shape, axis):
    return lax.broadcasted_iota(I32, shape, axis)


def onehot(mask):
    return jnp.where(mask, F32(1.0), F32(0.0)).astype(BF16)


def to_column(row, rows):
    mask = iota((rows, 128), 0) == iota((rows, 128), 1)
    return jnp.sum(jnp.where(mask, row, jnp.zeros((), row.dtype)), axis=1, keepdims=True)


def to_row(column):
    shape = (column.shape[0], 128)
    mask = iota(shape, 0) == iota(shape, 1)
    return jnp.sum(jnp.where(mask, column, jnp.zeros((), column.dtype)), axis=0, keepdims=True)


def backward(g, score, kept):
    gate_value, up_value = kept[:, :FF_DEV], kept[:, FF_DEV:]
    sigm = jax.nn.sigmoid(gate_value)
    activated = gate_value * sigm
    slope = sigm * (1.0 + gate_value * (1.0 - sigm))
    hidden = (activated * up_value).astype(BF16).astype(F32)
    inner = jnp.sum(hidden * g, axis=1, keepdims=True)
    hidden_grad = score * g
    hg = jnp.concatenate([hidden_grad * up_value * slope, hidden_grad * activated], axis=1).astype(BF16)
    return hg, inner


def kernel(sections, up_hbm, ids_ref, slots_ref, logits_ref, router_ref, kept_hbm, wgu_hbm, wd_hbm,
           fin_hbm, ft_hbm, rt_hbm, hgrad_hbm,
           up_v, kept_v, wgu_v, wd_v, wgut_v, wdt_v, perm_v, kp_v, hgp_v, x_v, xs_v, es_v, ein_v, eall_v, own_v, sbo_v, sbi_v, out_v,
           rel_v, dir_v, rto_v, rti_v, rts2_v, tl_v, inn_v, fino_v, fto_v, rts_v, hg_v,
           send_sem, recv_sem, sb_send, sb_recv, loc_sem):
    sec = lax.axis_index("section")
    me = lax.axis_index("expert")
    c = lax.rem(me, 2)
    y = lax.rem(me // 2, SIDE)
    x = me // (2 * SIDE)

    def dev(dx=0, dy=0, dc=0, dz=0):
        s = lax.rem(sec + dz + sections, sections)
        e = (lax.rem(x + dx + SIDE, SIDE) * SIDE + lax.rem(y + dy + SIDE, SIDE)) * 2 + lax.rem(c + dc, 2)
        return (s, e)

    table = {}
    for d in (1, 3, 2):
        table["x", d] = (xs_v.at[d - 1], x_v.at[SLOT[0, d], 0], dev(dx=-d))
        table["e", d] = (es_v.at[d], ein_v.at[d - 1], dev(dx=-d))
    for d in range(4):
        n0 = SLOT[0, d]
        table["y+", d] = (x_v.at[n0, 0], x_v.at[SLOT[3, d], 0], dev(dy=1))
        table["y-", d] = (x_v.at[n0, 0], x_v.at[SLOT[1, d], 0], dev(dy=-1))
        if d in PLUS:
            table["yr", d] = (x_v.at[SLOT[3, d], 0], x_v.at[SLOT[2, d], 0], dev(dy=1))
            table["rr", d] = (out_v.at[SLOT[2, d]], rel_v.at[d], dev(dy=1))
        else:
            table["yr", d] = (x_v.at[SLOT[1, d], 0], x_v.at[SLOT[2, d], 0], dev(dy=-1))
            table["rr", d] = (out_v.at[SLOT[2, d]], rel_v.at[d], dev(dy=-1))
        for k in range(4):
            n = SLOT[k, d]
            table["sib", k, d] = (x_v.at[n, 0], x_v.at[n, 1], dev(dc=1))
        for h in range(2):
            table["d+", d, h] = (out_v.at[SLOT[1, d], h], dir_v.at[0, d, h], dev(dy=1))
            table["d-", d, h] = (out_v.at[SLOT[3, d], h], dir_v.at[1, d, h], dev(dy=-1))
            table["f", d, h] = (fino_v.at[d, h], fin_hbm.at[h, d], dev(dx=d, dz=-1))
        table["ft", d] = (fto_v, ft_hbm.at[d], dev(dx=d, dz=-1))
    for k in range(4):
        table["es", k] = (eall_v.at[2 * k], eall_v.at[2 * k + 1], dev(dc=1))
        if k:
            table["ea", k] = (eall_v.at[0], eall_v.at[2 * ((4 - k) % 4)], dev(dy=k))
            table["rt", k] = (rto_v.at[0, k], rti_v.at[(4 - k) % 4], dev(dy=k))
    table[("rs",)] = (rto_v.at[1], rts2_v, dev(dc=1))
    table[("ids",)] = (rts_v, rt_hbm, dev(dz=-1))
    number = {name: i for i, name in enumerate(table)}

    def copy(*name):
        src, dst, device = table[name]
        i = number[name]
        return pltpu.make_async_remote_copy(
            src_ref=src, dst_ref=dst, send_sem=send_sem.at[i], recv_sem=recv_sem.at[i],
            device_id=device, device_id_type=pl.DeviceIdType.MESH)

    def start(*name):
        copy(*name).start()

    def recv(*name):
        copy(*name).wait_recv()

    got = set()

    def need(*name):
        if name not in got:
            recv(*name)
        got.add(name)

    up_copy = pltpu.make_async_copy(up_hbm, up_v, loc_sem.at[4])
    kept_copy = pltpu.make_async_copy(kept_hbm, kept_v, loc_sem.at[0])
    wd_copy = pltpu.make_async_copy(wd_hbm, wd_v, loc_sem.at[1])
    wgu_copy = pltpu.make_async_copy(wgu_hbm, wgu_v, loc_sem.at[2])
    up_copy.start()
    barrier = pltpu.get_barrier_semaphore()
    partners = [dev(dx=d) for d in (1, 2, 3)]
    partners += [dev(dy=k, dc=s) for k in range(4) for s in range(2) if k or s]
    partners += [dev(dx=d, dz=dz) for d in range(4) for dz in (-1, 1)]
    for partner in partners:
        pl.semaphore_signal(barrier, inc=1, device_id=partner, device_id_type=pl.DeviceIdType.MESH)

    wd_copy.start()
    kept_copy.start()
    wgu_copy.start()
    ids_row, slot_row = ids_ref[...], slots_ref[...]
    rel_row = jnp.bitwise_and(x + SIDE - ids_row, 3)
    key = jnp.where(slot_row < REG, rel_row * REG + slot_row, -1)
    perm = onehot(iota((TOK, TOK), 0) == key)
    up_copy.wait()
    up = up_v[...]
    rows = dot(perm, up).astype(BF16)
    x_v[SLOT[0, 0], 0] = rows[:REG]
    for d in range(1, 4):
        xs_v[d - 1] = rows[d * REG:(d + 1) * REG]
    ids_col, slot_col = to_column(ids_row, TOK), to_column(slot_row, TOK)
    chosen = jnp.sum(jnp.where(iota((SIDE, TOK), 0) == ids_row, logits_ref[...], 0.0), axis=0, keepdims=True)
    part = to_column(jax.nn.sigmoid(chosen), TOK)
    fold = jnp.zeros((4 * 16, QUART), F32)
    gates = jnp.zeros((4 * 16, 128), F32)
    for q in range(4):
        place = iota((4 * 16, TOK), 0) == rel_row * 17 + 4 * q
        fold += dot(onehot(place & (slot_row == REG)), up[:, q * QUART:(q + 1) * QUART])
        if q < 3:
            rounded = part.astype(BF16).astype(F32)
            spread = jnp.where(iota((TOK, 128), 1) == slot_col, rounded, 0.0).astype(BF16)
            gates += dot(onehot(place), spread)
            part = part - rounded
    tiles = jnp.concatenate([fold, gates], axis=1).astype(BF16)
    for d in range(4):
        es_v[d] = tiles[16 * d:16 * (d + 1)]
    rts_v[...] = jnp.concatenate([ids_row, slot_row, jnp.zeros((6, TOK), I32)], axis=0)

    def capacity(p):
        return jnp.where(p < 16 * REG, p // REG * MOST + jnp.bitwise_and(p, REG - 1), (p - 16 * REG) * MOST + REG)

    perm_v[...] = onehot(capacity(iota((PART, PART), 0)) == iota((PART, PART), 1))
    inn_v[...] = jnp.zeros_like(inn_v)
    pl.semaphore_wait(barrier, len(partners))
    def fold_tiles():
        for d in (1, 2, 3):
            need("e", d)
        tile = es_v[0].astype(F32)
        for d in (1, 2, 3):
            tile += ein_v[d - 1].astype(F32)
        eall_v[0] = tile.astype(BF16)

    def prepare():
        wd_copy.wait()
        for t in range(5):
            wdt_v[512 * t:512 * (t + 1), :] = wd_v[:, 512 * t:512 * (t + 1)].T
        kept_copy.wait()
        for p in range(2):
            for t in range(2):
                cols = slice(512 * t, 512 * (t + 1))
                kp_v[p, :, cols] = dot(perm_v[...], kept_v[PART * p:PART * (p + 1), cols]).astype(BF16)
        perm_v[...] = onehot(capacity(iota((PART, PART), 1)) == iota((PART, PART), 0))
        wgu_copy.wait()
        for t in range(5):
            wgut_v[:, 512 * t:512 * (t + 1)] = wgu_v[512 * t:512 * (t + 1), :].T

    def need_chunk(k, d):
        if k or d:
            need(*{0: ("x", d), 1: ("y-", d), 2: ("yr", d), 3: ("y+", d)}[k])

    def need_tiles(k):
        need("es", k)
        if k:
            need("ea", (4 - k) % 4)

    def half_copy(n):
        return pltpu.make_async_remote_copy(
            src_ref=sbo_v.at[n], dst_ref=sbi_v.at[n], send_sem=sb_send.at[n], recv_sem=sb_recv.at[n],
            device_id=dev(dc=1), device_id_type=pl.DeviceIdType.MESH)

    def finish(m):
        for j in range(2):
            n = 2 * m + j
            half_copy(n).wait_recv()
            both = own_v[n] + sbi_v[n].astype(F32)
            own_v[n] = both
            out_v[n] = both.astype(BF16)

    def select(q, flip):
        shape = (128, 32) if flip else (32, 128)
        b, place = iota(shape, 1 if flip else 0), iota(shape, 0 if flip else 1)
        idx = 2 * jnp.bitwise_and(b // 2 - y + SIDE, 3) + jnp.bitwise_and(b + c, 1)
        return onehot(place == idx * 16 + 4 * q + jnp.bitwise_and(b // 8 - x + SIDE, 3))

    def extras():
        for k in range(4):
            need_tiles(k)
        spread_tiles = eall_v[...].reshape(8 * 16, TILE_W)
        extra = jnp.concatenate([dot(select(q, False), spread_tiles[:, :QUART]).astype(BF16) for q in range(4)], axis=1)
        gate_rows = dot(select(0, False), spread_tiles[:, QUART:])
        score = jnp.sum(jnp.where(iota((32, 128), 1) == REG, gate_rows, 0.0), axis=1, keepdims=True)
        kept = kp_v[:, 16 * REG:, :].reshape(32, 2 * FF_DEV).astype(F32)
        hg, inner = backward(dot(extra, wdt_v[...]), score, kept)
        hgp_v[:, 16 * REG:, :] = hg.reshape(2, 16, 2 * FF_DEV)
        dx = dot(hg, wgut_v[...]).astype(BF16)
        folded = jnp.zeros((8 * 16, QUART), F32)
        for q in range(4):
            folded += dot(select(q, True), dx[:, q * QUART:(q + 1) * QUART])
        inner_at = jnp.where(iota((32, 128), 1) == REG, inner, 0.0).astype(BF16)
        tl_v[...] = jnp.concatenate([folded, dot(select(0, True), inner_at)], axis=1).astype(BF16)

    def tiles_back():
        inners = inn_v[...].reshape(8 * 16, 128) + tl_v[:, QUART:].astype(F32)
        tiles = jnp.concatenate([tl_v[:, :QUART], inners.astype(BF16)], axis=1).reshape(4, 2, 16, TILE_W)
        rto_v[0] = tiles[:, 0]
        rto_v[1] = tiles[:, 1]

    def add_tiles():
        if ("rs",) not in got:
            need("rs")
            rto_v[0] = (rto_v[0].astype(F32) + rts2_v[...].astype(F32)).astype(BF16)

    def restore():
        for p in range(2):
            for t in range(2):
                cols = slice(512 * t, 512 * (t + 1))
                kept_v[PART * p:PART * (p + 1), cols] = dot(perm_v[...], hgp_v[p, :, cols]).astype(BF16)
        hgrad_copy.start()

    hgrad_copy = pltpu.make_async_copy(kept_v, hgrad_hbm, loc_sem.at[3])
    w_row = jnp.sum(jnp.where(iota((SIDE, D), 0) == x, router_ref[...].astype(F32), 0.0), axis=0, keepdims=True)
    terms = []

    def totals():
        add_tiles()
        for k in (1, 2, 3):
            need("rt", k)
        total = rto_v[0, 0].astype(F32)
        for k in (1, 2, 3):
            total += rti_v[k].astype(F32)
        gate_tile = eall_v[0, :, QUART:].astype(F32)
        kind = jnp.bitwise_and(iota((16, 128), 0), 3)
        all_terms = jnp.zeros((16, 128), F32)
        for d in range(4):
            gate = jnp.sum(jnp.where(kind == d, gate_tile, 0.0), axis=0, keepdims=True)
            inner_row = jnp.sum(jnp.where(iota((16, 128), 0) == d, total[:, QUART:], 0.0), axis=0, keepdims=True)
            terms.append(gate * (1.0 - gate) * inner_row)
            all_terms = jnp.where(kind == d, terms[d], all_terms)
        last_term = jnp.sum(jnp.where(iota((16, 128), 1) == REG, all_terms, 0.0), axis=1, keepdims=True)
        w_fold = jnp.zeros((16, QUART), F32)
        for q in range(4):
            w_fold = jnp.where(iota((16, QUART), 0) // 4 == q, w_row[:, q * QUART:(q + 1) * QUART], w_fold)
        fto_v[...] = (total[:, :QUART] + last_term * w_fold).astype(BF16)

    def final(d, h):
        need("d+", d, h)
        need("d-", d, h)
        n = SLOT[0, d]
        rows = own_v[n, h] + dir_v[0, d, h].astype(F32) + dir_v[1, d, h].astype(F32)
        fino_v[d, h] = (rows + to_column(terms[d], REG) * w_row[:, HALF * h:HALF * (h + 1)]).astype(BF16)
        start("f", d, h)

    def act(kind, *at):
        if kind in ("y+", "y-") and at[0]:
            need("x", *at)
        elif kind == "yr":
            need("y+" if at[0] in PLUS else "y-", *at)
        elif kind == "sib":
            need_chunk(*at)
        elif kind == "es" and at[0]:
            need("ea", (4 - at[0]) % 4)
        elif kind in ("d+", "d-"):
            d, h = at
            if (d in PLUS) == (kind == "d+"):
                need("rr", d)
                n = SLOT[1 if kind == "d+" else 3, d]
                out_v[n, h] = (own_v[n, h] + rel_v[d, h].astype(F32)).astype(BF16)
        elif kind == "rs":
            tiles_back()
        elif kind == "rt":
            add_tiles()
        whole = {"E0": fold_tiles, "prep": prepare, "fin": finish, "ext": extras, "terms": totals, "final": final, "perm": restore}
        if kind in whole:
            whole[kind](*at)
        elif kind == "ft":
            for d in range(4):
                start("ft", d)
        else:
            start(kind, *at)

    parts = [[]]
    for entry in PLAN:
        if entry[0] == "out":
            continue
        if entry[0] == "step":
            parts.append([])
        else:
            parts[-1].append(entry)

    def before(i):
        for entry in parts[i]:
            act(*entry)
        for k, d in ORDER[2 * i:2 * i + 2]:
            need_chunk(k, d)
            need("sib", k, d)
            need_tiles(k)

    start("ids")
    before(0)

    @pl.loop(0, STEPS)
    def _(it):
        for i in range(1, STEPS):
            @pl.when(it == i)
            def _():
                before(i)

        rows = x_v[pl.ds(2 * it, 2)].reshape(4 * REG, D)
        g = dot(rows, wdt_v[...])
        for j in range(2):
            k, d = [jnp.bitwise_and(jnp.right_shift(jnp.int32(PACK[axis][j]), 2 * it), 3) for axis in range(2)]
            for s in range(2):
                at = (2 * j + s) * REG
                idx = 2 * k + s
                b = jnp.bitwise_and(x + d, 3) * 8 + jnp.bitwise_and(y + k, 3) * 2 + jnp.bitwise_and(c + s, 1)
                window = pl.ds(pl.multiple_of(jnp.bitwise_and(b, 15) * REG, REG), REG)
                kept = kp_v[b // 16, window, :].astype(F32)
                line = iota((16, 128), 0) == d
                score_row = jnp.sum(jnp.where(line, eall_v[idx, :, QUART:].astype(F32), 0.0), axis=0, keepdims=True)
                hg, inner = backward(g[at:at + REG], to_column(score_row, REG), kept)
                hg_v[at:at + REG, :] = hg
                inn_v[idx] = jnp.where(line, to_row(inner), inn_v[idx])
                hgp_v[b // 16, window, :] = hg
        for h in range(2):
            dx = dot(hg_v[...], wgut_v[:, HALF * h:HALF * (h + 1)])
            for j in range(2):
                own_v[2 * it + j, h] = dx[2 * j * REG:(2 * j + 1) * REG]
                sbo_v[2 * it + j, h] = dx[(2 * j + 1) * REG:(2 * j + 2) * REG].astype(BF16)
        for j in range(2):
            half_copy(2 * it + j).start()

    for entry in parts[STEPS]:
        act(*entry)

    need("ids")
    for d in range(4):
        need("ft", d)
        for h in range(2):
            need("f", d, h)
    for name in table:
        copy(*name).wait_send()
    for n in range(2 * STEPS):
        half_copy(n).wait_send()
    hgrad_copy.wait()


def assemble(sections, fin_hbm, ft_hbm, rt_hbm, hg_hbm, prev_hbm, hgrad_hbm, fin_v, ft_v, rt_v, hg_v, prev_v, sem):
    x = lax.axis_index("expert") // (2 * SIDE)
    live = lax.axis_index("section") < sections - 1
    into = [pltpu.make_async_copy(a, b, sem.at[i]) for i, (a, b) in enumerate(
        ((rt_hbm, rt_v), (ft_hbm, ft_v), (fin_hbm.at[0], fin_v.at[0]), (fin_hbm.at[1], fin_v.at[1])))]
    span = SLOTS // 3
    part = [pl.ds(span * i, span) for i in range(3)]
    hg_in = [pltpu.make_async_copy(hg_hbm.at[p], hg_v.at[p], sem.at[4 + i]) for i, p in enumerate(part)]
    hg_out = [pltpu.make_async_copy(hg_v.at[p], hgrad_hbm.at[p], sem.at[7 + i]) for i, p in enumerate(part)]
    prev_out = [pltpu.make_async_copy(prev_v.at[h], prev_hbm.at[:, pl.ds(h * HALF, HALF)], sem.at[10 + h]) for h in range(2)]
    for copy in into + hg_in:
        copy.start()
    for copy in into[:2]:
        copy.wait()
    ids_col, slot_col = to_column(rt_v[0:1, :], TOK), to_column(rt_v[1:2, :], TOK)
    rel_col = jnp.bitwise_and(x + SIDE - ids_col, 3)
    back = onehot((iota((TOK, TOK), 1) == jnp.where(slot_col < REG, rel_col * REG + slot_col, -1)) & live)
    fts = ft_v[...].reshape(4 * 16, QUART)
    for h in range(2):
        into[2 + h].wait()
        whole = dot(back, fin_v[h].reshape(TOK, HALF))
        extra = []
        for q in (2 * h, 2 * h + 1):
            pick = onehot((iota((TOK, 4 * 16), 1) == jnp.where(slot_col == REG, rel_col * 17 + 4 * q, -1)) & live)
            extra.append(dot(pick, fts))
        prev_v[h] = (whole + jnp.concatenate(extra, axis=1)).astype(BF16)
        prev_out[h].start()
        hg_in[h].wait()
        hg_out[h].start()
    hg_in[2].wait()
    hg_out[2].start()
    for copy in prev_out + hg_out:
        copy.wait()


def on_device(out_grad, expert_ids, slot_ids, router_logits, saved_routed, w_gate_up, w_down, w_router):
    sections = lax.axis_size("section")
    vmem = pl.BlockSpec(memory_space=pltpu.VMEM)
    hbm = pl.BlockSpec(memory_space=pl.ANY)

    def body(*refs):
        kernel(sections, *refs)

    count = 96
    fin, ft, rt, hg = pl.pallas_call(
        body,
        out_shape=(
            jax.ShapeDtypeStruct((2, 4, REG, HALF), BF16),
            jax.ShapeDtypeStruct((4, 16, QUART), BF16),
            jax.ShapeDtypeStruct((8, TOK), I32),
            jax.ShapeDtypeStruct((SLOTS, 2 * FF_DEV), BF16),
        ),
        in_specs=[hbm] + [vmem] * 4 + [hbm] * 3,
        out_specs=(hbm,) * 4,
        scratch_shapes=[
            pltpu.VMEM((TOK, D), BF16),
            pltpu.VMEM((SLOTS, 2 * FF_DEV), BF16),
            pltpu.VMEM((D, 2 * FF_DEV), BF16),
            pltpu.VMEM((FF_DEV, D), BF16),
            pltpu.VMEM((2 * FF_DEV, D), BF16),
            pltpu.VMEM((D, FF_DEV), BF16),
            pltpu.VMEM((PART, PART), BF16),
            pltpu.VMEM((2, PART, 2 * FF_DEV), BF16),
            pltpu.VMEM((2, PART, 2 * FF_DEV), BF16),
            pltpu.VMEM((16, 2, REG, D), BF16),
            pltpu.VMEM((3, REG, D), BF16),
            pltpu.VMEM((4, 16, TILE_W), BF16),
            pltpu.VMEM((3, 16, TILE_W), BF16),
            pltpu.VMEM((8, 16, TILE_W), BF16),
            pltpu.VMEM((16, 2, REG, HALF), F32),
            pltpu.VMEM((16, 2, REG, HALF), BF16),
            pltpu.VMEM((16, 2, REG, HALF), BF16),
            pltpu.VMEM((16, 2, REG, HALF), BF16),
            pltpu.VMEM((4, 2, REG, HALF), BF16),
            pltpu.VMEM((2, 4, 2, REG, HALF), BF16),
            pltpu.VMEM((2, 4, 16, TILE_W), BF16),
            pltpu.VMEM((4, 16, TILE_W), BF16),
            pltpu.VMEM((4, 16, TILE_W), BF16),
            pltpu.VMEM((8 * 16, TILE_W), BF16),
            pltpu.VMEM((8, 16, 128), F32),
            pltpu.VMEM((4, 2, REG, HALF), BF16),
            pltpu.VMEM((16, QUART), BF16),
            pltpu.VMEM((8, TOK), I32),
            pltpu.VMEM((4 * REG, 2 * FF_DEV), BF16),
            pltpu.SemaphoreType.DMA((count,)),
            pltpu.SemaphoreType.DMA((count,)),
            pltpu.SemaphoreType.DMA((16,)),
            pltpu.SemaphoreType.DMA((16,)),
            pltpu.SemaphoreType.DMA((5,)),
        ],
        compiler_params=pltpu.CompilerParams(collective_id=0, has_side_effects=True, vmem_limit_bytes=60 * 2**20),
        cost_estimate=pl.CostEstimate(flops=9 * 10**9, bytes_accessed=14 * 10**6, transcendentals=600000),
    )(out_grad[0], expert_ids, slot_ids, router_logits[0].T, w_router[0].T, saved_routed[0, 0], w_gate_up[0, 0], w_down[0, 0])

    def last(*refs):
        assemble(sections, *refs)

    prev, hgrad = pl.pallas_call(
        last,
        out_shape=(jax.ShapeDtypeStruct((TOK, D), BF16), jax.ShapeDtypeStruct((SLOTS, 2 * FF_DEV), BF16)),
        in_specs=[hbm] * 4,
        out_specs=(hbm, hbm),
        scratch_shapes=[
            pltpu.VMEM((2, 4, REG, HALF), BF16),
            pltpu.VMEM((4, 16, QUART), BF16),
            pltpu.VMEM((8, TOK), I32),
            pltpu.VMEM((SLOTS, 2 * FF_DEV), BF16),
            pltpu.VMEM((2, TOK, HALF), BF16),
            pltpu.SemaphoreType.DMA((12,)),
        ],
        compiler_params=pltpu.CompilerParams(vmem_limit_bytes=60 * 2**20),
        cost_estimate=pl.CostEstimate(flops=10**8, bytes_accessed=6 * 10**6, transcendentals=0),
    )(fin, ft, rt, hg)
    return prev[None], hgrad[None, None]


def solution(mesh):
    placed = (
        P("section", "expert", None),
        P("section", "expert"),
        P("section", "expert"),
        P("section", "expert", None),
        P("section", "expert", None, None),
        P("section", "expert", None, None),
        P("section", "expert", None, None),
        P("section", None, None),
    )
    return jax.shard_map(
        on_device,
        mesh=mesh,
        in_specs=placed,
        out_specs=(P("section", "expert", None), P("section", "expert", None, None)),
        check_vma=False,
    )
```

```python
import jax
import jax.numpy as jnp
from jax import lax
from jax.experimental import pallas as pl
from jax.experimental.pallas import tpu as pltpu
from jax.sharding import PartitionSpec as P

F32, BF16, I32 = jnp.float32, jnp.bfloat16, jnp.int32
SIDE = 4
TOK = 128
MOST = 33
REG = 32
D = 2560
FF_DEV = 512
SLOTS = 1056
QUART = D // 4
TILE_W = QUART + 128
HALF = D // 2
PART = 528

ORDER = [
    (3, 0), (3, 1), (0, 1), (2, 0), (1, 3), (1, 0), (2, 3), (2, 1), (1, 2), (0, 0), (0, 2), (0, 3), (3, 2), (1, 1),
    (2, 2), (3, 3),
]
SLOT = {chunk: i for i, chunk in enumerate(ORDER)}
PLAN = [
    ("x", 3, 0), ("x", 1, 1), ("y+", 0, 0), ("y-", 0, 0), ("x", 1, 0), ("y+", 0, 1), ("x", 3, 1), ("y-", 0, 1),
    ("e", 2), ("prep",), ("y-", 3, 0), ("y+", 1, 1), ("e", 3), ("e", 1), ("x", 2, 1), ("sib", 0, 3), ("y+", 1, 0),
    ("y-", 3, 1), ("sib", 3, 0), ("E0",), ("y-", 1, 1), ("ea", 1), ("es", 0), ("ea", 3), ("ea", 2), ("yr", 0),
    ("x", 2, 0), ("sib", 3, 1), ("sib", 1, 0), ("yr", 3), ("y-", 2, 1), ("yr", 1), ("sib", 1, 3), ("y+", 2, 1),
    ("es", 3), ("step", 0), ("y+", 3, 1), ("es", 2), ("y+", 2, 0), ("y+", 3, 0), ("sib", 0, 0), ("y-", 2, 0), ("es", 1),
    ("y-", 1, 0), ("sib", 0, 2), ("sib", 2, 0), ("sib", 0, 1), ("fin", 0), ("ext",), ("step", 1), ("sib", 2, 3),
    ("sib", 2, 1), ("step", 2), ("yr", 2), ("sib", 1, 2), ("step", 3), ("step", 4), ("fin", 3), ("rr", 3), ("rr", 1),
    ("sib", 3, 2), ("d-", 1, 1), ("d-", 1, 0), ("sib", 1, 1), ("step", 5), ("fin", 1), ("rr", 0), ("sib", 2, 2),
    ("sib", 3, 3), ("step", 6), ("step", 7), ("rs",), ("fin", 5), ("rt", 2), ("rt", 3), ("rt", 1), ("fin", 4),
    ("fin", 7), ("d-", 3, 0), ("rr", 2), ("fin", 6), ("fin", 2), ("d-", 3, 1), ("d+", 3, 0), ("d-", 0, 1), ("d+", 1, 1),
    ("d+", 1, 0), ("terms",), ("ft",), ("d+", 3, 1), ("d+", 0, 1), ("final", 3, 0), ("d+", 2, 0), ("final", 1, 1),
    ("final", 1, 0), ("d-", 2, 0), ("final", 3, 1), ("d+", 2, 1), ("d-", 2, 1), ("final", 0, 1), ("d-", 0, 0),
    ("d+", 0, 0), ("final", 2, 0), ("perm",), ("final", 2, 1), ("final", 0, 0),
]
STEPS = 8
PLUS = (0, 1)


def packed(values):
    return sum(v << (2 * i) for i, v in enumerate(values))


PACK = [[packed([ORDER[2 * i + j][axis] for i in range(STEPS)]) for j in range(2)] for axis in range(2)]


def dot(a, b):
    return lax.dot_general(a, b, (((1,), (0,)), ((), ())), preferred_element_type=F32)


def iota(shape, axis):
    return lax.broadcasted_iota(I32, shape, axis)


def onehot(mask):
    return jnp.where(mask, F32(1.0), F32(0.0)).astype(BF16)


def to_column(row, rows):
    mask = iota((rows, 128), 0) == iota((rows, 128), 1)
    return jnp.sum(jnp.where(mask, row, jnp.zeros((), row.dtype)), axis=1, keepdims=True)


def to_row(column):
    shape = (column.shape[0], 128)
    mask = iota(shape, 0) == iota(shape, 1)
    return jnp.sum(jnp.where(mask, column, jnp.zeros((), column.dtype)), axis=0, keepdims=True)


def backward(g, score, kept):
    gate_value, up_value = kept[:, :FF_DEV], kept[:, FF_DEV:]
    sigm = jax.nn.sigmoid(gate_value)
    activated = gate_value * sigm
    slope = sigm * (1.0 + gate_value * (1.0 - sigm))
    hidden = (activated * up_value).astype(BF16).astype(F32)
    inner = jnp.sum(hidden * g, axis=1, keepdims=True)
    hidden_grad = score * g
    hg = jnp.concatenate([hidden_grad * up_value * slope, hidden_grad * activated], axis=1).astype(BF16)
    return hg, inner


def kernel(sections, up_hbm, ids_ref, slots_ref, logits_ref, router_ref, kept_hbm, wgu_hbm, wd_hbm,
           fin_hbm, ft_hbm, rt_hbm, hgrad_hbm,
           up_v, kept_v, wgu_v, wd_v, wgut_v, wdt_v, perm_v, kp_v, hgp_v, x_v, xs_v, es_v, ein_v, eall_v, own_v, sbo_v, sbi_v, out_v,
           rel_v, dir_v, rto_v, rti_v, rts2_v, tl_v, inn_v, fino_v, fto_v, rts_v, hg_v,
           send_sem, recv_sem, sb_send, sb_recv, loc_sem):
    sec = lax.axis_index("section")
    me = lax.axis_index("expert")
    c = lax.rem(me, 2)
    y = lax.rem(me // 2, SIDE)
    x = me // (2 * SIDE)

    def dev(dx=0, dy=0, dc=0, dz=0):
        s = lax.rem(sec + dz + sections, sections)
        e = (lax.rem(x + dx + SIDE, SIDE) * SIDE + lax.rem(y + dy + SIDE, SIDE)) * 2 + lax.rem(c + dc, 2)
        return (s, e)

    table = {}
    for d in (1, 3, 2):
        for part in range(2):
            half = pl.ds(16 * part, 16)
            table["x", d, part] = (xs_v.at[d - 1, half], x_v.at[SLOT[0, d], 0, half], dev(dx=-d))
        table["e", d] = (es_v.at[d], ein_v.at[d - 1], dev(dx=-d))
    for d in range(4):
        n0 = SLOT[0, d]
        for part in range(2):
            half = pl.ds(16 * part, 16)
            table["y+", d, part] = (x_v.at[n0, 0, half], x_v.at[SLOT[3, d], 0, half], dev(dy=1))
            table["y-", d, part] = (x_v.at[n0, 0, half], x_v.at[SLOT[1, d], 0, half], dev(dy=-1))
        if d in PLUS:
            table["yr", d] = (x_v.at[SLOT[3, d], 0], x_v.at[SLOT[2, d], 0], dev(dy=1))
            table["rr", d] = (out_v.at[SLOT[2, d]], rel_v.at[d], dev(dy=1))
        else:
            table["yr", d] = (x_v.at[SLOT[1, d], 0], x_v.at[SLOT[2, d], 0], dev(dy=-1))
            table["rr", d] = (out_v.at[SLOT[2, d]], rel_v.at[d], dev(dy=-1))
        for k in range(4):
            n = SLOT[k, d]
            table["sib", k, d] = (x_v.at[n, 0], x_v.at[n, 1], dev(dc=1))
        for h in range(2):
            table["d+", d, h] = (out_v.at[SLOT[1, d], h], dir_v.at[0, d, h], dev(dy=1))
            table["d-", d, h] = (out_v.at[SLOT[3, d], h], dir_v.at[1, d, h], dev(dy=-1))
            table["f", d, h] = (fino_v.at[d, h], fin_hbm.at[h, d], dev(dx=d, dz=-1))
        table["ft", d] = (fto_v, ft_hbm.at[d], dev(dx=d, dz=-1))
    for k in range(4):
        table["es", k] = (eall_v.at[2 * k], eall_v.at[2 * k + 1], dev(dc=1))
        if k:
            table["ea", k] = (eall_v.at[0], eall_v.at[2 * ((4 - k) % 4)], dev(dy=k))
            table["rt", k] = (rto_v.at[0, k], rti_v.at[(4 - k) % 4], dev(dy=k))
    table[("rs",)] = (rto_v.at[1], rts2_v, dev(dc=1))
    table[("ids",)] = (rts_v, rt_hbm, dev(dz=-1))
    number = {name: i for i, name in enumerate(table)}

    def copy(*name):
        src, dst, device = table[name]
        i = number[name]
        return pltpu.make_async_remote_copy(
            src_ref=src, dst_ref=dst, send_sem=send_sem.at[i], recv_sem=recv_sem.at[i],
            device_id=device, device_id_type=pl.DeviceIdType.MESH)

    def start(*name):
        copy(*name).start()

    def recv(*name):
        copy(*name).wait_recv()

    got = set()

    def need(*name):
        if name not in got:
            recv(*name)
        got.add(name)

    up_copy = pltpu.make_async_copy(up_hbm, up_v, loc_sem.at[4])
    kept_copy = pltpu.make_async_copy(kept_hbm, kept_v, loc_sem.at[0])
    wd_copy = pltpu.make_async_copy(wd_hbm, wd_v, loc_sem.at[1])
    wgu_copy = pltpu.make_async_copy(wgu_hbm, wgu_v, loc_sem.at[2])
    up_copy.start()
    barrier = pltpu.get_barrier_semaphore()
    partners = [dev(dx=d) for d in (1, 2, 3)]
    partners += [dev(dy=k, dc=s) for k in range(4) for s in range(2) if k or s]
    partners += [dev(dx=d, dz=dz) for d in range(4) for dz in (-1, 1)]
    for partner in partners:
        pl.semaphore_signal(barrier, inc=1, device_id=partner, device_id_type=pl.DeviceIdType.MESH)

    wd_copy.start()
    kept_copy.start()
    wgu_copy.start()
    ids_row, slot_row = ids_ref[...], slots_ref[...]
    rel_row = jnp.bitwise_and(x + SIDE - ids_row, 3)
    key = jnp.where(slot_row < REG, rel_row * REG + slot_row, -1)
    perm = onehot(iota((TOK, TOK), 0) == key)
    up_copy.wait()
    up = up_v[...]
    rows = dot(perm, up).astype(BF16)
    x_v[SLOT[0, 0], 0] = rows[:REG]
    for d in range(1, 4):
        xs_v[d - 1] = rows[d * REG:(d + 1) * REG]
    ids_col, slot_col = to_column(ids_row, TOK), to_column(slot_row, TOK)
    chosen = jnp.sum(jnp.where(iota((SIDE, TOK), 0) == ids_row, logits_ref[...], 0.0), axis=0, keepdims=True)
    part = to_column(jax.nn.sigmoid(chosen), TOK)
    fold = jnp.zeros((4 * 16, QUART), F32)
    gates = jnp.zeros((4 * 16, 128), F32)
    for q in range(4):
        place = iota((4 * 16, TOK), 0) == rel_row * 17 + 4 * q
        fold += dot(onehot(place & (slot_row == REG)), up[:, q * QUART:(q + 1) * QUART])
        if q < 3:
            rounded = part.astype(BF16).astype(F32)
            spread = jnp.where(iota((TOK, 128), 1) == slot_col, rounded, 0.0).astype(BF16)
            gates += dot(onehot(place), spread)
            part = part - rounded
    tiles = jnp.concatenate([fold, gates], axis=1).astype(BF16)
    for d in range(4):
        es_v[d] = tiles[16 * d:16 * (d + 1)]
    rts_v[...] = jnp.concatenate([ids_row, slot_row, jnp.zeros((6, TOK), I32)], axis=0)

    def capacity(p):
        return jnp.where(p < 16 * REG, p // REG * MOST + jnp.bitwise_and(p, REG - 1), (p - 16 * REG) * MOST + REG)

    perm_v[...] = onehot(capacity(iota((PART, PART), 0)) == iota((PART, PART), 1))
    inn_v[...] = jnp.zeros_like(inn_v)
    pl.semaphore_wait(barrier, len(partners))
    def fold_tiles():
        for d in (1, 2, 3):
            need("e", d)
        tile = es_v[0].astype(F32)
        for d in (1, 2, 3):
            tile += ein_v[d - 1].astype(F32)
        eall_v[0] = tile.astype(BF16)

    def prepare():
        wd_copy.wait()
        for t in range(5):
            wdt_v[512 * t:512 * (t + 1), :] = wd_v[:, 512 * t:512 * (t + 1)].T
        kept_copy.wait()
        for p in range(2):
            for t in range(2):
                cols = slice(512 * t, 512 * (t + 1))
                kp_v[p, :, cols] = dot(perm_v[...], kept_v[PART * p:PART * (p + 1), cols]).astype(BF16)
        perm_v[...] = onehot(capacity(iota((PART, PART), 1)) == iota((PART, PART), 0))
        wgu_copy.wait()
        for t in range(5):
            wgut_v[:, 512 * t:512 * (t + 1)] = wgu_v[512 * t:512 * (t + 1), :].T

    def need_chunk(k, d):
        if k == 2:
            need("yr", d)
        elif k or d:
            for part in range(2):
                need({0: "x", 1: "y-", 3: "y+"}[k], d, part)

    def need_tiles(k):
        need("es", k)
        if k:
            need("ea", (4 - k) % 4)

    def half_copy(n):
        return pltpu.make_async_remote_copy(
            src_ref=sbo_v.at[n], dst_ref=sbi_v.at[n], send_sem=sb_send.at[n], recv_sem=sb_recv.at[n],
            device_id=dev(dc=1), device_id_type=pl.DeviceIdType.MESH)

    def finish(m):
        for j in range(2):
            n = 2 * m + j
            half_copy(n).wait_recv()
            both = own_v[n] + sbi_v[n].astype(F32)
            own_v[n] = both
            out_v[n] = both.astype(BF16)

    def select(q, flip):
        shape = (128, 32) if flip else (32, 128)
        b, place = iota(shape, 1 if flip else 0), iota(shape, 0 if flip else 1)
        idx = 2 * jnp.bitwise_and(b // 2 - y + SIDE, 3) + jnp.bitwise_and(b + c, 1)
        return onehot(place == idx * 16 + 4 * q + jnp.bitwise_and(b // 8 - x + SIDE, 3))

    def extras():
        for k in range(4):
            need_tiles(k)
        spread_tiles = eall_v[...].reshape(8 * 16, TILE_W)
        extra = jnp.concatenate([dot(select(q, False), spread_tiles[:, :QUART]).astype(BF16) for q in range(4)], axis=1)
        gate_rows = dot(select(0, False), spread_tiles[:, QUART:])
        score = jnp.sum(jnp.where(iota((32, 128), 1) == REG, gate_rows, 0.0), axis=1, keepdims=True)
        kept = kp_v[:, 16 * REG:, :].reshape(32, 2 * FF_DEV).astype(F32)
        hg, inner = backward(dot(extra, wdt_v[...]), score, kept)
        hgp_v[:, 16 * REG:, :] = hg.reshape(2, 16, 2 * FF_DEV)
        dx = dot(hg, wgut_v[...]).astype(BF16)
        folded = jnp.zeros((8 * 16, QUART), F32)
        for q in range(4):
            folded += dot(select(q, True), dx[:, q * QUART:(q + 1) * QUART])
        inner_at = jnp.where(iota((32, 128), 1) == REG, inner, 0.0).astype(BF16)
        tl_v[...] = jnp.concatenate([folded, dot(select(0, True), inner_at)], axis=1).astype(BF16)

    def tiles_back():
        inners = inn_v[...].reshape(8 * 16, 128) + tl_v[:, QUART:].astype(F32)
        tiles = jnp.concatenate([tl_v[:, :QUART], inners.astype(BF16)], axis=1).reshape(4, 2, 16, TILE_W)
        rto_v[0] = tiles[:, 0]
        rto_v[1] = tiles[:, 1]

    def add_tiles():
        if ("rs",) not in got:
            need("rs")
            rto_v[0] = (rto_v[0].astype(F32) + rts2_v[...].astype(F32)).astype(BF16)

    def restore():
        for p in range(2):
            for t in range(2):
                cols = slice(512 * t, 512 * (t + 1))
                kept_v[PART * p:PART * (p + 1), cols] = dot(perm_v[...], hgp_v[p, :, cols]).astype(BF16)
        hgrad_copy.start()

    hgrad_copy = pltpu.make_async_copy(kept_v, hgrad_hbm, loc_sem.at[3])
    w_row = jnp.sum(jnp.where(iota((SIDE, D), 0) == x, router_ref[...].astype(F32), 0.0), axis=0, keepdims=True)
    terms = []

    def totals():
        add_tiles()
        for k in (1, 2, 3):
            need("rt", k)
        total = rto_v[0, 0].astype(F32)
        for k in (1, 2, 3):
            total += rti_v[k].astype(F32)
        gate_tile = eall_v[0, :, QUART:].astype(F32)
        kind = jnp.bitwise_and(iota((16, 128), 0), 3)
        all_terms = jnp.zeros((16, 128), F32)
        for d in range(4):
            gate = jnp.sum(jnp.where(kind == d, gate_tile, 0.0), axis=0, keepdims=True)
            inner_row = jnp.sum(jnp.where(iota((16, 128), 0) == d, total[:, QUART:], 0.0), axis=0, keepdims=True)
            terms.append(gate * (1.0 - gate) * inner_row)
            all_terms = jnp.where(kind == d, terms[d], all_terms)
        last_term = jnp.sum(jnp.where(iota((16, 128), 1) == REG, all_terms, 0.0), axis=1, keepdims=True)
        w_fold = jnp.zeros((16, QUART), F32)
        for q in range(4):
            w_fold = jnp.where(iota((16, QUART), 0) // 4 == q, w_row[:, q * QUART:(q + 1) * QUART], w_fold)
        fto_v[...] = (total[:, :QUART] + last_term * w_fold).astype(BF16)

    def final(d, h):
        need("d+", d, h)
        need("d-", d, h)
        n = SLOT[0, d]
        rows = own_v[n, h] + dir_v[0, d, h].astype(F32) + dir_v[1, d, h].astype(F32)
        fino_v[d, h] = (rows + to_column(terms[d], REG) * w_row[:, HALF * h:HALF * (h + 1)]).astype(BF16)
        start("f", d, h)

    def act(kind, *at):
        if kind in ("y+", "y-") and at[0]:
            need("x", *at)
        elif kind == "yr":
            need_chunk(3 if at[0] in PLUS else 1, *at)
        elif kind == "sib":
            need_chunk(*at)
        elif kind == "es" and at[0]:
            need("ea", (4 - at[0]) % 4)
        elif kind in ("d+", "d-"):
            d, h = at
            if (d in PLUS) == (kind == "d+"):
                need("rr", d)
                n = SLOT[1 if kind == "d+" else 3, d]
                out_v[n, h] = (own_v[n, h] + rel_v[d, h].astype(F32)).astype(BF16)
        elif kind == "rs":
            tiles_back()
        elif kind == "rt":
            add_tiles()
        whole = {"E0": fold_tiles, "prep": prepare, "fin": finish, "ext": extras, "terms": totals, "final": final, "perm": restore}
        if kind in whole:
            whole[kind](*at)
        elif kind == "ft":
            for d in range(4):
                start("ft", d)
        else:
            start(kind, *at)

    parts = [[]]
    for entry in PLAN:
        if entry[0] == "out":
            continue
        if entry[0] == "step":
            parts.append([])
        else:
            parts[-1].append(entry)

    def before(i):
        for entry in parts[i]:
            act(*entry)
        for k, d in ORDER[2 * i:2 * i + 2]:
            need_chunk(k, d)
            need("sib", k, d)
            need_tiles(k)

    start("ids")
    before(0)

    @pl.loop(0, STEPS)
    def _(it):
        for i in range(1, STEPS):
            @pl.when(it == i)
            def _():
                before(i)

        rows = x_v[pl.ds(2 * it, 2)].reshape(4 * REG, D)
        g = dot(rows, wdt_v[...])
        for j in range(2):
            k, d = [jnp.bitwise_and(jnp.right_shift(jnp.int32(PACK[axis][j]), 2 * it), 3) for axis in range(2)]
            for s in range(2):
                at = (2 * j + s) * REG
                idx = 2 * k + s
                b = jnp.bitwise_and(x + d, 3) * 8 + jnp.bitwise_and(y + k, 3) * 2 + jnp.bitwise_and(c + s, 1)
                window = pl.ds(pl.multiple_of(jnp.bitwise_and(b, 15) * REG, REG), REG)
                kept = kp_v[b // 16, window, :].astype(F32)
                line = iota((16, 128), 0) == d
                score_row = jnp.sum(jnp.where(line, eall_v[idx, :, QUART:].astype(F32), 0.0), axis=0, keepdims=True)
                hg, inner = backward(g[at:at + REG], to_column(score_row, REG), kept)
                hg_v[at:at + REG, :] = hg
                inn_v[idx] = jnp.where(line, to_row(inner), inn_v[idx])
                hgp_v[b // 16, window, :] = hg
        for h in range(2):
            dx = dot(hg_v[...], wgut_v[:, HALF * h:HALF * (h + 1)])
            for j in range(2):
                own_v[2 * it + j, h] = dx[2 * j * REG:(2 * j + 1) * REG]
                sbo_v[2 * it + j, h] = dx[(2 * j + 1) * REG:(2 * j + 2) * REG].astype(BF16)
        for j in range(2):
            half_copy(2 * it + j).start()

    for entry in parts[STEPS]:
        act(*entry)

    need("ids")
    for d in range(4):
        need("ft", d)
        for h in range(2):
            need("f", d, h)
    for name in table:
        copy(*name).wait_send()
    for n in range(2 * STEPS):
        half_copy(n).wait_send()
    hgrad_copy.wait()


def assemble(sections, fin_v, ft_v, rt_v, hg_any, prev_hbm, hgrad_hbm, prev_v, sem):
    x = lax.axis_index("expert") // (2 * SIDE)
    live = lax.axis_index("section") < sections - 1
    span = SLOTS // 3
    part = [pl.ds(span * i, span) for i in range(3)]
    out = [pltpu.make_async_copy(hg_any.at[p], hgrad_hbm.at[p], sem.at[2 + i]) for i, p in enumerate(part)]
    prev_out = [pltpu.make_async_copy(prev_v.at[h], prev_hbm.at[:, pl.ds(h * HALF, HALF)], sem.at[h]) for h in range(2)]
    for copy in out:
        copy.start()
    ids_col, slot_col = to_column(rt_v[0:1, :], TOK), to_column(rt_v[1:2, :], TOK)
    rel_col = jnp.bitwise_and(x + SIDE - ids_col, 3)
    back = onehot((iota((TOK, TOK), 1) == jnp.where(slot_col < REG, rel_col * REG + slot_col, -1)) & live)
    fts = ft_v[...].reshape(4 * 16, QUART)
    for h in range(2):
        whole = dot(back, fin_v[h].reshape(TOK, HALF))
        extra = []
        for q in (2 * h, 2 * h + 1):
            pick = onehot((iota((TOK, 4 * 16), 1) == jnp.where(slot_col == REG, rel_col * 17 + 4 * q, -1)) & live)
            extra.append(dot(pick, fts))
        prev_v[h] = (whole + jnp.concatenate(extra, axis=1)).astype(BF16)
        prev_out[h].start()
    for copy in prev_out + out:
        copy.wait()


def on_device(out_grad, expert_ids, slot_ids, router_logits, saved_routed, w_gate_up, w_down, w_router):
    sections = lax.axis_size("section")
    vmem = pl.BlockSpec(memory_space=pltpu.VMEM)
    hbm = pl.BlockSpec(memory_space=pl.ANY)

    def body(*refs):
        kernel(sections, *refs)

    count = 96
    fin, ft, rt, hg = pl.pallas_call(
        body,
        out_shape=(
            pltpu.VMEM((2, 4, REG, HALF), BF16),
            pltpu.VMEM((4, 16, QUART), BF16),
            pltpu.VMEM((8, TOK), I32),
            pltpu.VMEM((SLOTS, 2 * FF_DEV), BF16),
        ),
        in_specs=[hbm] + [vmem] * 4 + [hbm] * 3,
        out_specs=(hbm,) * 4,
        scratch_shapes=[
            pltpu.VMEM((TOK, D), BF16),
            pltpu.VMEM((SLOTS, 2 * FF_DEV), BF16),
            pltpu.VMEM((D, 2 * FF_DEV), BF16),
            pltpu.VMEM((FF_DEV, D), BF16),
            pltpu.VMEM((2 * FF_DEV, D), BF16),
            pltpu.VMEM((D, FF_DEV), BF16),
            pltpu.VMEM((PART, PART), BF16),
            pltpu.VMEM((2, PART, 2 * FF_DEV), BF16),
            pltpu.VMEM((2, PART, 2 * FF_DEV), BF16),
            pltpu.VMEM((16, 2, REG, D), BF16),
            pltpu.VMEM((3, REG, D), BF16),
            pltpu.VMEM((4, 16, TILE_W), BF16),
            pltpu.VMEM((3, 16, TILE_W), BF16),
            pltpu.VMEM((8, 16, TILE_W), BF16),
            pltpu.VMEM((16, 2, REG, HALF), F32),
            pltpu.VMEM((16, 2, REG, HALF), BF16),
            pltpu.VMEM((16, 2, REG, HALF), BF16),
            pltpu.VMEM((16, 2, REG, HALF), BF16),
            pltpu.VMEM((4, 2, REG, HALF), BF16),
            pltpu.VMEM((2, 4, 2, REG, HALF), BF16),
            pltpu.VMEM((2, 4, 16, TILE_W), BF16),
            pltpu.VMEM((4, 16, TILE_W), BF16),
            pltpu.VMEM((4, 16, TILE_W), BF16),
            pltpu.VMEM((8 * 16, TILE_W), BF16),
            pltpu.VMEM((8, 16, 128), F32),
            pltpu.VMEM((4, 2, REG, HALF), BF16),
            pltpu.VMEM((16, QUART), BF16),
            pltpu.VMEM((8, TOK), I32),
            pltpu.VMEM((4 * REG, 2 * FF_DEV), BF16),
            pltpu.SemaphoreType.DMA((count,)),
            pltpu.SemaphoreType.DMA((count,)),
            pltpu.SemaphoreType.DMA((16,)),
            pltpu.SemaphoreType.DMA((16,)),
            pltpu.SemaphoreType.DMA((5,)),
        ],
        compiler_params=pltpu.CompilerParams(collective_id=0, has_side_effects=True, vmem_limit_bytes=56 * 2**20),
        cost_estimate=pl.CostEstimate(flops=9 * 10**9, bytes_accessed=14 * 10**6, transcendentals=600000),
    )(out_grad[0], expert_ids, slot_ids, router_logits[0].T, w_router[0].T, saved_routed[0, 0], w_gate_up[0, 0], w_down[0, 0])

    def last(*refs):
        assemble(sections, *refs)

    held = [pltpu.with_memory_space_constraint(a, pltpu.VMEM) for a in (fin, ft, rt, hg)]
    prev, hgrad = pl.pallas_call(
        last,
        out_shape=(jax.ShapeDtypeStruct((TOK, D), BF16), jax.ShapeDtypeStruct((SLOTS, 2 * FF_DEV), BF16)),
        in_specs=[vmem] * 3 + [hbm],
        out_specs=(hbm, hbm),
        scratch_shapes=[
            pltpu.VMEM((2, TOK, HALF), BF16),
            pltpu.SemaphoreType.DMA((5,)),
        ],
        compiler_params=pltpu.CompilerParams(vmem_limit_bytes=32 * 2**20),
        cost_estimate=pl.CostEstimate(flops=10**8, bytes_accessed=6 * 10**6, transcendentals=0),
    )(*held)
    return prev[None], hgrad[None, None]


def solution(mesh):
    placed = (
        P("section", "expert", None),
        P("section", "expert"),
        P("section", "expert"),
        P("section", "expert", None),
        P("section", "expert", None, None),
        P("section", "expert", None, None),
        P("section", "expert", None, None),
        P("section", None, None),
    )
    return jax.shard_map(
        on_device,
        mesh=mesh,
        in_specs=placed,
        out_specs=(P("section", "expert", None), P("section", "expert", None, None)),
        check_vma=False,
    )
```

```python
import jax
import jax.numpy as jnp
from jax import lax
from jax.experimental import pallas as pl
from jax.experimental.pallas import tpu as pltpu
from jax.sharding import PartitionSpec as P

F32, BF16, I32 = jnp.float32, jnp.bfloat16, jnp.int32
SIDE = 4
TOK = 128
MOST = 33
REG = 32
D = 2560
FF_DEV = 512
SLOTS = 1056
QUART = D // 4
TILE_W = QUART + 128
HALF = D // 2
PART = 528

ORDER = [
    (0, 0), (0, 1), (1, 3), (1, 0), (3, 0), (0, 2), (2, 0), (3, 1), (2, 1), (2, 3), (1, 2), (0, 3), (3, 3), (1, 1),
    (3, 2), (2, 2),
]
SLOT = {chunk: i for i, chunk in enumerate(ORDER)}
PLAN = [
    ("x", 1), ("x", 3), ("y+", 0), ("y-", 0), ("e", 1), ("sib", 0, 0), ("e", 3), ("e", 2), ("x", 2), ("prep",),
    ("sib", 0, 3), ("y+", 1), ("y-", 3), ("E0",), ("ea", 2), ("ea", 1), ("yr", 0), ("ea", 3), ("es", 0), ("y-", 2),
    ("sib", 0, 1), ("yr", 1), ("sib", 3, 1), ("y+", 3), ("sib", 1, 0), ("sib", 0, 2), ("yr", 3), ("es", 2), ("es", 3),
    ("y+", 2), ("es", 1), ("sib", 1, 3), ("sib", 3, 0), ("y-", 1), ("step", 0), ("step", 1), ("sib", 2, 0), ("yr", 2),
    ("sib", 1, 2), ("step", 2), ("ext",), ("sib", 2, 1), ("sib", 2, 3), ("step", 3), ("step", 4), ("sib", 1, 1),
    ("fin", 3), ("d-", 1, 0), ("rr", 0), ("sib", 3, 3), ("step", 5), ("fin", 2), ("d-", 1, 1), ("fin", 4), ("rr", 1),
    ("rr", 3), ("fin", 1), ("sib", 3, 2), ("sib", 2, 2), ("step", 6), ("step", 7), ("rs",), ("rt", 2), ("rt", 1),
    ("rt", 3), ("d-", 0, 1), ("fin", 6), ("fin", 0), ("d+", 0, 1), ("fin", 7), ("d+", 1, 0), ("rr", 2), ("d+", 1, 1),
    ("terms",), ("d-", 0, 0), ("ft",), ("d+", 0, 0), ("final", 0, 1), ("d+", 3, 1), ("d-", 3, 1), ("d-", 3, 0),
    ("d+", 3, 0), ("final", 1, 0), ("fin", 5), ("final", 1, 1), ("d-", 2, 1), ("final", 0, 0), ("d+", 2, 1),
    ("d-", 2, 0), ("d+", 2, 0), ("final", 3, 1), ("final", 3, 0), ("final", 2, 1), ("final", 2, 0), ("perm",),
    ("out", 1), ("out", 0),
]
STEPS = 8
PLUS = (0, 1)


def packed(values):
    return sum(v << (2 * i) for i, v in enumerate(values))


PACK = [[packed([ORDER[2 * i + j][axis] for i in range(STEPS)]) for j in range(2)] for axis in range(2)]


def dot(a, b):
    return lax.dot_general(a, b, (((1,), (0,)), ((), ())), preferred_element_type=F32)


def iota(shape, axis):
    return lax.broadcasted_iota(I32, shape, axis)


def onehot(mask):
    return jnp.where(mask, F32(1.0), F32(0.0)).astype(BF16)


def to_column(row, rows):
    mask = iota((rows, 128), 0) == iota((rows, 128), 1)
    return jnp.sum(jnp.where(mask, row, jnp.zeros((), row.dtype)), axis=1, keepdims=True)


def to_row(column):
    shape = (column.shape[0], 128)
    mask = iota(shape, 0) == iota(shape, 1)
    return jnp.sum(jnp.where(mask, column, jnp.zeros((), column.dtype)), axis=0, keepdims=True)


def backward(g, score, kept):
    gate_value, up_value = kept[:, :FF_DEV], kept[:, FF_DEV:]
    sigm = jax.nn.sigmoid(gate_value)
    activated = gate_value * sigm
    slope = sigm * (1.0 + gate_value * (1.0 - sigm))
    hidden = (activated * up_value).astype(BF16).astype(F32)
    inner = jnp.sum(hidden * g, axis=1, keepdims=True)
    hidden_grad = score * g
    hg = jnp.concatenate([hidden_grad * up_value * slope, hidden_grad * activated], axis=1).astype(BF16)
    return hg, inner


def kernel(sections, up_hbm, ids_ref, slots_ref, logits_ref, router_ref, kept_hbm, wgu_hbm, wd_hbm,
           fin_hbm, ft_hbm, rt_hbm, hgrad_hbm,
           up_v, kept_v, wgu_v, wd_v, wgut_v, wdt_v, perm_v, kp_v, hgp_v, x_v, xs_v, es_v, ein_v, eall_v, own_v, sbo_v, sbi_v, out_v,
           rel_v, dir_v, rto_v, rti_v, rts2_v, tl_v, inn_v, fino_v, fto_v, rts_v, hg_v,
           send_sem, recv_sem, sb_send, sb_recv, loc_sem):
    sec = lax.axis_index("section")
    me = lax.axis_index("expert")
    c = lax.rem(me, 2)
    y = lax.rem(me // 2, SIDE)
    x = me // (2 * SIDE)

    def dev(dx=0, dy=0, dc=0, dz=0):
        s = lax.rem(sec + dz + sections, sections)
        e = (lax.rem(x + dx + SIDE, SIDE) * SIDE + lax.rem(y + dy + SIDE, SIDE)) * 2 + lax.rem(c + dc, 2)
        return (s, e)

    table = {}
    for d in (1, 3, 2):
        table["x", d] = (xs_v.at[d - 1], x_v.at[SLOT[0, d], 0], dev(dx=-d))
        table["e", d] = (es_v.at[d], ein_v.at[d - 1], dev(dx=-d))
    for d in range(4):
        n0 = SLOT[0, d]
        table["y+", d] = (x_v.at[n0, 0], x_v.at[SLOT[3, d], 0], dev(dy=1))
        table["y-", d] = (x_v.at[n0, 0], x_v.at[SLOT[1, d], 0], dev(dy=-1))
        if d in PLUS:
            table["yr", d] = (x_v.at[SLOT[3, d], 0], x_v.at[SLOT[2, d], 0], dev(dy=1))
            table["rr", d] = (out_v.at[SLOT[2, d]], rel_v.at[d], dev(dy=1))
        else:
            table["yr", d] = (x_v.at[SLOT[1, d], 0], x_v.at[SLOT[2, d], 0], dev(dy=-1))
            table["rr", d] = (out_v.at[SLOT[2, d]], rel_v.at[d], dev(dy=-1))
        for k in range(4):
            n = SLOT[k, d]
            table["sib", k, d] = (x_v.at[n, 0], x_v.at[n, 1], dev(dc=1))
        for h in range(2):
            table["d+", d, h] = (out_v.at[SLOT[1, d], h], dir_v.at[0, d, h], dev(dy=1))
            table["d-", d, h] = (out_v.at[SLOT[3, d], h], dir_v.at[1, d, h], dev(dy=-1))
            table["f", d, h] = (fino_v.at[d, h], fin_hbm.at[h, d], dev(dx=d, dz=-1))
        table["ft", d] = (fto_v, ft_hbm.at[d], dev(dx=d, dz=-1))
    for k in range(4):
        table["es", k] = (eall_v.at[2 * k], eall_v.at[2 * k + 1], dev(dc=1))
        if k:
            table["ea", k] = (eall_v.at[0], eall_v.at[2 * ((4 - k) % 4)], dev(dy=k))
            table["rt", k] = (rto_v.at[0, k], rti_v.at[(4 - k) % 4], dev(dy=k))
    table[("rs",)] = (rto_v.at[1], rts2_v, dev(dc=1))
    table[("ids",)] = (rts_v, rt_hbm, dev(dz=-1))
    number = {name: i for i, name in enumerate(table)}

    def copy(*name):
        src, dst, device = table[name]
        i = number[name]
        return pltpu.make_async_remote_copy(
            src_ref=src, dst_ref=dst, send_sem=send_sem.at[i], recv_sem=recv_sem.at[i],
            device_id=device, device_id_type=pl.DeviceIdType.MESH)

    def start(*name):
        copy(*name).start()

    def recv(*name):
        copy(*name).wait_recv()

    got = set()

    def need(*name):
        if name not in got:
            recv(*name)
        got.add(name)

    up_copy = pltpu.make_async_copy(up_hbm, up_v, loc_sem.at[4])
    kept_copy = pltpu.make_async_copy(kept_hbm, kept_v, loc_sem.at[0])
    wd_copy = pltpu.make_async_copy(wd_hbm, wd_v, loc_sem.at[1])
    wgu_copy = pltpu.make_async_copy(wgu_hbm, wgu_v, loc_sem.at[2])
    up_copy.start()
    barrier = pltpu.get_barrier_semaphore()
    partners = [dev(dx=d) for d in (1, 2, 3)]
    partners += [dev(dy=k, dc=s) for k in range(4) for s in range(2) if k or s]
    partners += [dev(dx=d, dz=dz) for d in range(4) for dz in (-1, 1)]
    for partner in partners:
        pl.semaphore_signal(barrier, inc=1, device_id=partner, device_id_type=pl.DeviceIdType.MESH)

    wd_copy.start()
    kept_copy.start()
    wgu_copy.start()
    ids_row, slot_row = ids_ref[...], slots_ref[...]
    rel_row = jnp.bitwise_and(x + SIDE - ids_row, 3)
    key = jnp.where(slot_row < REG, rel_row * REG + slot_row, -1)
    perm = onehot(iota((TOK, TOK), 0) == key)
    up_copy.wait()
    up = up_v[...]
    rows = dot(perm, up).astype(BF16)
    x_v[SLOT[0, 0], 0] = rows[:REG]
    for d in range(1, 4):
        xs_v[d - 1] = rows[d * REG:(d + 1) * REG]
    ids_col, slot_col = to_column(ids_row, TOK), to_column(slot_row, TOK)
    chosen = jnp.sum(jnp.where(iota((SIDE, TOK), 0) == ids_row, logits_ref[...], 0.0), axis=0, keepdims=True)
    part = to_column(jax.nn.sigmoid(chosen), TOK)
    fold = jnp.zeros((4 * 16, QUART), F32)
    gates = jnp.zeros((4 * 16, 128), F32)
    for q in range(4):
        place = iota((4 * 16, TOK), 0) == rel_row * 17 + 4 * q
        fold += dot(onehot(place & (slot_row == REG)), up[:, q * QUART:(q + 1) * QUART])
        if q < 3:
            rounded = part.astype(BF16).astype(F32)
            spread = jnp.where(iota((TOK, 128), 1) == slot_col, rounded, 0.0).astype(BF16)
            gates += dot(onehot(place), spread)
            part = part - rounded
    tiles = jnp.concatenate([fold, gates], axis=1).astype(BF16)
    for d in range(4):
        es_v[d] = tiles[16 * d:16 * (d + 1)]
    rts_v[...] = jnp.concatenate([ids_row, slot_row, jnp.zeros((6, TOK), I32)], axis=0)

    def capacity(p):
        return jnp.where(p < 16 * REG, p // REG * MOST + jnp.bitwise_and(p, REG - 1), (p - 16 * REG) * MOST + REG)

    perm_v[...] = onehot(capacity(iota((PART, PART), 0)) == iota((PART, PART), 1))
    inn_v[...] = jnp.zeros_like(inn_v)
    pl.semaphore_wait(barrier, len(partners))
    def fold_tiles():
        for d in (1, 2, 3):
            need("e", d)
        tile = es_v[0].astype(F32)
        for d in (1, 2, 3):
            tile += ein_v[d - 1].astype(F32)
        eall_v[0] = tile.astype(BF16)

    def prepare():
        wd_copy.wait()
        for t in range(5):
            wdt_v[512 * t:512 * (t + 1), :] = wd_v[:, 512 * t:512 * (t + 1)].T
        kept_copy.wait()
        for p in range(2):
            for t in range(2):
                cols = slice(512 * t, 512 * (t + 1))
                kp_v[p, :, cols] = dot(perm_v[...], kept_v[PART * p:PART * (p + 1), cols]).astype(BF16)
        perm_v[...] = onehot(capacity(iota((PART, PART), 1)) == iota((PART, PART), 0))
        wgu_copy.wait()
        for t in range(5):
            wgut_v[:, 512 * t:512 * (t + 1)] = wgu_v[512 * t:512 * (t + 1), :].T

    def need_chunk(k, d):
        if k or d:
            need({0: "x", 1: "y-", 2: "yr", 3: "y+"}[k], d)

    def need_tiles(k):
        need("es", k)
        if k:
            need("ea", (4 - k) % 4)

    def half_copy(n):
        return pltpu.make_async_remote_copy(
            src_ref=sbo_v.at[n], dst_ref=sbi_v.at[n], send_sem=sb_send.at[n], recv_sem=sb_recv.at[n],
            device_id=dev(dc=1), device_id_type=pl.DeviceIdType.MESH)

    def finish(m):
        for j in range(2):
            n = 2 * m + j
            half_copy(n).wait_recv()
            both = own_v[n] + sbi_v[n].astype(F32)
            own_v[n] = both
            out_v[n] = both.astype(BF16)

    def select(q, flip):
        shape = (128, 32) if flip else (32, 128)
        b, place = iota(shape, 1 if flip else 0), iota(shape, 0 if flip else 1)
        idx = 2 * jnp.bitwise_and(b // 2 - y + SIDE, 3) + jnp.bitwise_and(b + c, 1)
        return onehot(place == idx * 16 + 4 * q + jnp.bitwise_and(b // 8 - x + SIDE, 3))

    def extras():
        for k in range(4):
            need_tiles(k)
        spread_tiles = eall_v[...].reshape(8 * 16, TILE_W)
        extra = jnp.concatenate([dot(select(q, False), spread_tiles[:, :QUART]).astype(BF16) for q in range(4)], axis=1)
        gate_rows = dot(select(0, False), spread_tiles[:, QUART:])
        score = jnp.sum(jnp.where(iota((32, 128), 1) == REG, gate_rows, 0.0), axis=1, keepdims=True)
        kept = kp_v[:, 16 * REG:, :].reshape(32, 2 * FF_DEV).astype(F32)
        hg, inner = backward(dot(extra, wdt_v[...]), score, kept)
        hgp_v[:, 16 * REG:, :] = hg.reshape(2, 16, 2 * FF_DEV)
        dx = dot(hg, wgut_v[...]).astype(BF16)
        folded = jnp.zeros((8 * 16, QUART), F32)
        for q in range(4):
            folded += dot(select(q, True), dx[:, q * QUART:(q + 1) * QUART])
        inner_at = jnp.where(iota((32, 128), 1) == REG, inner, 0.0).astype(BF16)
        tl_v[...] = jnp.concatenate([folded, dot(select(0, True), inner_at)], axis=1).astype(BF16)

    def tiles_back():
        inners = inn_v[...].reshape(8 * 16, 128) + tl_v[:, QUART:].astype(F32)
        tiles = jnp.concatenate([tl_v[:, :QUART], inners.astype(BF16)], axis=1).reshape(4, 2, 16, TILE_W)
        rto_v[0] = tiles[:, 0]
        rto_v[1] = tiles[:, 1]

    def add_tiles():
        if ("rs",) not in got:
            need("rs")
            rto_v[0] = (rto_v[0].astype(F32) + rts2_v[...].astype(F32)).astype(BF16)

    def restore():
        for p in range(2):
            for t in range(2):
                cols = slice(512 * t, 512 * (t + 1))
                kept_v[PART * p:PART * (p + 1), cols] = dot(perm_v[...], hgp_v[p, :, cols]).astype(BF16)
        hgrad_copy.start()

    hgrad_copy = pltpu.make_async_copy(kept_v, hgrad_hbm, loc_sem.at[3])
    w_row = jnp.sum(jnp.where(iota((SIDE, D), 0) == x, router_ref[...].astype(F32), 0.0), axis=0, keepdims=True)
    terms = []

    def totals():
        add_tiles()
        for k in (1, 2, 3):
            need("rt", k)
        total = rto_v[0, 0].astype(F32)
        for k in (1, 2, 3):
            total += rti_v[k].astype(F32)
        gate_tile = eall_v[0, :, QUART:].astype(F32)
        kind = jnp.bitwise_and(iota((16, 128), 0), 3)
        all_terms = jnp.zeros((16, 128), F32)
        for d in range(4):
            gate = jnp.sum(jnp.where(kind == d, gate_tile, 0.0), axis=0, keepdims=True)
            inner_row = jnp.sum(jnp.where(iota((16, 128), 0) == d, total[:, QUART:], 0.0), axis=0, keepdims=True)
            terms.append(gate * (1.0 - gate) * inner_row)
            all_terms = jnp.where(kind == d, terms[d], all_terms)
        last_term = jnp.sum(jnp.where(iota((16, 128), 1) == REG, all_terms, 0.0), axis=1, keepdims=True)
        w_fold = jnp.zeros((16, QUART), F32)
        for q in range(4):
            w_fold = jnp.where(iota((16, QUART), 0) // 4 == q, w_row[:, q * QUART:(q + 1) * QUART], w_fold)
        fto_v[...] = (total[:, :QUART] + last_term * w_fold).astype(BF16)

    def final(d, h):
        need("d+", d, h)
        need("d-", d, h)
        n = SLOT[0, d]
        rows = own_v[n, h] + dir_v[0, d, h].astype(F32) + dir_v[1, d, h].astype(F32)
        fino_v[d, h] = (rows + to_column(terms[d], REG) * w_row[:, HALF * h:HALF * (h + 1)]).astype(BF16)
        start("f", d, h)

    def act(kind, *at):
        if kind in ("y+", "y-") and at[0]:
            need("x", *at)
        elif kind == "yr":
            need_chunk(3 if at[0] in PLUS else 1, *at)
        elif kind == "sib":
            need_chunk(*at)
        elif kind == "es" and at[0]:
            need("ea", (4 - at[0]) % 4)
        elif kind in ("d+", "d-"):
            d, h = at
            if (d in PLUS) == (kind == "d+"):
                need("rr", d)
                n = SLOT[1 if kind == "d+" else 3, d]
                out_v[n, h] = (own_v[n, h] + rel_v[d, h].astype(F32)).astype(BF16)
        elif kind == "rs":
            tiles_back()
        elif kind == "rt":
            add_tiles()
        whole = {"E0": fold_tiles, "prep": prepare, "fin": finish, "ext": extras, "terms": totals, "final": final, "perm": restore}
        if kind in whole:
            whole[kind](*at)
        elif kind == "ft":
            for d in range(4):
                start("ft", d)
        else:
            start(kind, *at)

    parts = [[]]
    for entry in PLAN:
        if entry[0] == "out":
            continue
        if entry[0] == "step":
            parts.append([])
        else:
            parts[-1].append(entry)

    def before(i):
        for entry in parts[i]:
            act(*entry)
        for k, d in ORDER[2 * i:2 * i + 2]:
            need_chunk(k, d)
            need("sib", k, d)
            need_tiles(k)

    start("ids")
    before(0)

    @pl.loop(0, STEPS)
    def _(it):
        for i in range(1, STEPS):
            @pl.when(it == i)
            def _():
                before(i)

        rows = x_v[pl.ds(2 * it, 2)].reshape(4 * REG, D)
        g = dot(rows, wdt_v[...])
        for j in range(2):
            k, d = [jnp.bitwise_and(jnp.right_shift(jnp.int32(PACK[axis][j]), 2 * it), 3) for axis in range(2)]
            for s in range(2):
                at = (2 * j + s) * REG
                idx = 2 * k + s
                b = jnp.bitwise_and(x + d, 3) * 8 + jnp.bitwise_and(y + k, 3) * 2 + jnp.bitwise_and(c + s, 1)
                window = pl.ds(pl.multiple_of(jnp.bitwise_and(b, 15) * REG, REG), REG)
                kept = kp_v[b // 16, window, :].astype(F32)
                line = iota((16, 128), 0) == d
                score_row = jnp.sum(jnp.where(line, eall_v[idx, :, QUART:].astype(F32), 0.0), axis=0, keepdims=True)
                hg, inner = backward(g[at:at + REG], to_column(score_row, REG), kept)
                hg_v[at:at + REG, :] = hg
                inn_v[idx] = jnp.where(line, to_row(inner), inn_v[idx])
                hgp_v[b // 16, window, :] = hg
        for h in range(2):
            dx = dot(hg_v[...], wgut_v[:, HALF * h:HALF * (h + 1)])
            for j in range(2):
                own_v[2 * it + j, h] = dx[2 * j * REG:(2 * j + 1) * REG]
                sbo_v[2 * it + j, h] = dx[(2 * j + 1) * REG:(2 * j + 2) * REG].astype(BF16)
        for j in range(2):
            half_copy(2 * it + j).start()

    for entry in parts[STEPS]:
        act(*entry)

    need("ids")
    for d in range(4):
        need("ft", d)
        for h in range(2):
            need("f", d, h)
    for name in table:
        copy(*name).wait_send()
    for n in range(2 * STEPS):
        half_copy(n).wait_send()
    hgrad_copy.wait()


def assemble(sections, fin_v, ft_v, rt_v, hg_any, prev_hbm, hgrad_hbm, prev_v, sem):
    x = lax.axis_index("expert") // (2 * SIDE)
    live = lax.axis_index("section") < sections - 1
    span = SLOTS // 3
    part = [pl.ds(span * i, span) for i in range(3)]
    out = [pltpu.make_async_copy(hg_any.at[p], hgrad_hbm.at[p], sem.at[2 + i]) for i, p in enumerate(part)]
    prev_out = [pltpu.make_async_copy(prev_v.at[h], prev_hbm.at[:, pl.ds(h * HALF, HALF)], sem.at[h]) for h in range(2)]
    for copy in out:
        copy.start()
    ids_col, slot_col = to_column(rt_v[0:1, :], TOK), to_column(rt_v[1:2, :], TOK)
    rel_col = jnp.bitwise_and(x + SIDE - ids_col, 3)
    back = onehot((iota((TOK, TOK), 1) == jnp.where(slot_col < REG, rel_col * REG + slot_col, -1)) & live)
    fts = ft_v[...].reshape(4 * 16, QUART)
    for h in range(2):
        whole = dot(back, fin_v[h].reshape(TOK, HALF))
        extra = []
        for q in (2 * h, 2 * h + 1):
            pick = onehot((iota((TOK, 4 * 16), 1) == jnp.where(slot_col == REG, rel_col * 17 + 4 * q, -1)) & live)
            extra.append(dot(pick, fts))
        prev_v[h] = (whole + jnp.concatenate(extra, axis=1)).astype(BF16)
        prev_out[h].start()
    for copy in prev_out + out:
        copy.wait()


def on_device(out_grad, expert_ids, slot_ids, router_logits, saved_routed, w_gate_up, w_down, w_router):
    sections = lax.axis_size("section")
    vmem = pl.BlockSpec(memory_space=pltpu.VMEM)
    hbm = pl.BlockSpec(memory_space=pl.ANY)

    def body(*refs):
        kernel(sections, *refs)

    count = 96
    fin, ft, rt, hg = pl.pallas_call(
        body,
        out_shape=(
            pltpu.VMEM((2, 4, REG, HALF), BF16),
            pltpu.VMEM((4, 16, QUART), BF16),
            pltpu.VMEM((8, TOK), I32),
            pltpu.VMEM((SLOTS, 2 * FF_DEV), BF16),
        ),
        in_specs=[hbm] + [vmem] * 4 + [hbm] * 3,
        out_specs=(hbm,) * 4,
        scratch_shapes=[
            pltpu.VMEM((TOK, D), BF16),
            pltpu.VMEM((SLOTS, 2 * FF_DEV), BF16),
            pltpu.VMEM((D, 2 * FF_DEV), BF16),
            pltpu.VMEM((FF_DEV, D), BF16),
            pltpu.VMEM((2 * FF_DEV, D), BF16),
            pltpu.VMEM((D, FF_DEV), BF16),
            pltpu.VMEM((PART, PART), BF16),
            pltpu.VMEM((2, PART, 2 * FF_DEV), BF16),
            pltpu.VMEM((2, PART, 2 * FF_DEV), BF16),
            pltpu.VMEM((16, 2, REG, D), BF16),
            pltpu.VMEM((3, REG, D), BF16),
            pltpu.VMEM((4, 16, TILE_W), BF16),
            pltpu.VMEM((3, 16, TILE_W), BF16),
            pltpu.VMEM((8, 16, TILE_W), BF16),
            pltpu.VMEM((16, 2, REG, HALF), F32),
            pltpu.VMEM((16, 2, REG, HALF), BF16),
            pltpu.VMEM((16, 2, REG, HALF), BF16),
            pltpu.VMEM((16, 2, REG, HALF), BF16),
            pltpu.VMEM((4, 2, REG, HALF), BF16),
            pltpu.VMEM((2, 4, 2, REG, HALF), BF16),
            pltpu.VMEM((2, 4, 16, TILE_W), BF16),
            pltpu.VMEM((4, 16, TILE_W), BF16),
            pltpu.VMEM((4, 16, TILE_W), BF16),
            pltpu.VMEM((8 * 16, TILE_W), BF16),
            pltpu.VMEM((8, 16, 128), F32),
            pltpu.VMEM((4, 2, REG, HALF), BF16),
            pltpu.VMEM((16, QUART), BF16),
            pltpu.VMEM((8, TOK), I32),
            pltpu.VMEM((4 * REG, 2 * FF_DEV), BF16),
            pltpu.SemaphoreType.DMA((count,)),
            pltpu.SemaphoreType.DMA((count,)),
            pltpu.SemaphoreType.DMA((16,)),
            pltpu.SemaphoreType.DMA((16,)),
            pltpu.SemaphoreType.DMA((5,)),
        ],
        compiler_params=pltpu.CompilerParams(collective_id=0, has_side_effects=True, vmem_limit_bytes=56 * 2**20),
        cost_estimate=pl.CostEstimate(flops=9 * 10**9, bytes_accessed=14 * 10**6, transcendentals=600000),
    )(out_grad[0], expert_ids, slot_ids, router_logits[0].T, w_router[0].T, saved_routed[0, 0], w_gate_up[0, 0], w_down[0, 0])

    def last(*refs):
        assemble(sections, *refs)

    held = [pltpu.with_memory_space_constraint(a, pltpu.VMEM) for a in (fin, ft, rt, hg)]
    prev, hgrad = pl.pallas_call(
        last,
        out_shape=(jax.ShapeDtypeStruct((TOK, D), BF16), jax.ShapeDtypeStruct((SLOTS, 2 * FF_DEV), BF16)),
        in_specs=[vmem] * 3 + [hbm],
        out_specs=(hbm, hbm),
        scratch_shapes=[
            pltpu.VMEM((2, TOK, HALF), BF16),
            pltpu.SemaphoreType.DMA((5,)),
        ],
        compiler_params=pltpu.CompilerParams(vmem_limit_bytes=32 * 2**20),
        cost_estimate=pl.CostEstimate(flops=10**8, bytes_accessed=6 * 10**6, transcendentals=0),
    )(*held)
    return prev[None], hgrad[None, None]


def solution(mesh):
    placed = (
        P("section", "expert", None),
        P("section", "expert"),
        P("section", "expert"),
        P("section", "expert", None),
        P("section", "expert", None, None),
        P("section", "expert", None, None),
        P("section", "expert", None, None),
        P("section", None, None),
    )
    return jax.shard_map(
        on_device,
        mesh=mesh,
        in_specs=placed,
        out_specs=(P("section", "expert", None), P("section", "expert", None, None)),
        check_vma=False,
    )
```
